32 devices in a mesh: grp: 4 (over y, core), emb: 8 (over z, x).
Axes of the slice: x: 2, y: 2, z: 4, core: 2. Of those that a mesh axis runs over, the one named last changes fastest.
Arguments:
- table_window: bfloat16 [16384, 128], P('emb'), may hold values from -3 to 3
- dense_part: bfloat16 [4096, 128], P(('grp', 'emb')), may hold values from -6 to 6
- bag_rows: int32 [4096, 26, 8], P(('grp', 'emb')), may hold values from 0 to 2047
- bag_lengths: int32 [4096, 26], P(('grp', 'emb')), may hold values from 1 to 8
- bag_owner: int32 [4096, 26, 1], P(('grp', 'emb')), may hold values from 0 to 7; in each aligned block of 3328 rows (0 to 3327, 3328 to 6655, ..., all dimensions but the last counted through in order) at most 624 rows name the same one
- labels: int32 [4096], P(('grp', 'emb')), may hold values 0 or 1
- sample_weight: float32 [4096], P(('grp', 'emb')), may hold values from 0.005 to 1.5
- down_w: bfloat16 [3456, 512], replicated, may hold values from -0.109375 to 0.109375
- up_w: bfloat16 [512, 3456], replicated, may hold values from -0.25 to 0.25
- cross_bias: float32 [3456], replicated, may hold values from -3 to 3
- head_w: float32 [3456], replicated, may hold values from -0.109375 to 0.109375
Outputs:
- row_grad: float32 [16384, 128], P('emb')
- head_grad: float32 [3456], replicated
- bias_grad: float32 [3456], replicated
- dense_grad: bfloat16 [4096, 128], P(('grp', 'emb'))
The draws below stay inside these ranges and needn't reach their ends.
Inputs may be any that keep to these rules, and one draw needn't show every extreme that they name: `bag_owner`: among the bags of the samples of one device (aligned blocks of 128 samples), at most 624 have one owner, and some owner has exactly 624.
All inputs are finite; a program needn't handle non-finite values. No bound on the sum of `labels` on one device may be relied on, other than what follows from the above.
Results may differ from the reference program's by a relative error of at most 0.0045.
The reference program's roundings to bfloat16 on the way (of `pooled`, `x0`, `low`, `d_cross`, `d_low` and `d_pooled`) count: a program that leaves them out, or rounds other values in their place, can miss the bound.
Values may be sent and summed in bfloat16 or wider, within the bound.
No kernel may reach another device: no remote copies, remote signals or barrier semaphores. Data moves between devices by JAX's collectives and lax.ppermute only.
A program may use at most 128 MiB of HBM per device.

```python
import math
import jax
import jax.numpy as jnp
import numpy as np
from jax import lax

D_EMB = 128
TABLES = 26
RANK = 512
HOT = 8
SAMP = 128
LOCAL_ROWS = 2048
CROSS = 3456
CAP = 624
BATCH = 4096
WINDOW = 16384
N_EMB = 8


def draw_sample_weight(key, part):
    key = jax.random.fold_in(key, 11)
    position = jnp.arange(BATCH, dtype=jnp.float32) / BATCH
    falling = jnp.exp(-math.log(100.0) * position)
    jitter = jax.random.uniform(key, (BATCH,), jnp.float32, 0.7, 1.3)
    return (falling * jitter).astype(jnp.float32)


def set_ends(result, stream_key, low, high):
    spot = [jax.random.randint(jax.random.fold_in(stream_key, axis), (), 0, length) for axis, length in enumerate(result.shape)]
    main_axis = result.shape.index(max(result.shape))
    beside = spot[:main_axis] + [(spot[main_axis] + 1) % result.shape[main_axis]] + spot[main_axis + 1:]
    return result.at[tuple(spot)].set(low).at[tuple(beside)].set(high)


def levels(own_key, extent, pieces, smallest, largest):
    level, own = 1.0, jax.random.fold_in(own_key, 6)
    for dim, parts in pieces:
        steps = jnp.exp(jax.random.uniform(jax.random.fold_in(own, dim), (parts,), jnp.float32, smallest / len(pieces), largest / len(pieces)))
        level = level * jnp.repeat(steps, extent[dim] // parts).reshape([-1 if axis == dim else 1 for axis in range(len(extent))])
    return level


def routed_block(own_key, own, number, rows, count, top, reach, skew):
    ranking = jax.random.permutation(own_key, count)
    heavy_load, usual = load_shares(count, rows * top, reach, skew, True), load_shares(count, rows * top, reach, skew, False)
    places = jnp.arange(count)

    def named(tallies, rotation):
        used = int((tallies > 0).sum())
        fixed = max(1, used // 4)
        moved = fixed + (places - fixed + rotation * (used - fixed)) % max(1, count - fixed)
        return jnp.zeros((count,), jnp.int32).at[ranking[jnp.where(places < fixed, places, moved)]].set(jnp.asarray(tallies, jnp.int32))

    tallies = jnp.where(number % 4 == 0, named(heavy_load, number // 4), named(usual, number - number // 4 - 1))
    mixed = jax.random.permutation(jax.random.fold_in(own, 3), count)
    source_of, taker = mixed[0:count // 2 * 2:2], mixed[1:count // 2 * 2:2]
    margin = jnp.minimum(tallies[source_of] - 1, reach - tallies[taker]) // 2
    margin = jnp.where((source_of == ranking[0]) | (taker == ranking[0]) | (tallies[taker] == 0), 0, jnp.maximum(margin, 0))
    moved = jax.random.randint(jax.random.fold_in(own, 4), (count // 2,), 0, 1 << 20) % (margin + 1)
    tallies = tallies.at[source_of].add(-moved).at[taker].add(moved)
    items = jnp.searchsorted(jnp.cumsum(tallies), jnp.arange(rows * top), side="right").astype(jnp.int32)
    grid = items.reshape(top, rows).T
    grid = grid[jax.random.permutation(jax.random.fold_in(own, 1), rows)]
    rotation = jax.random.randint(jax.random.fold_in(own, 2), (rows, 1), 0, top)
    return jnp.take_along_axis(grid, (jnp.arange(top)[None, :] + rotation) % top, axis=1)


def load_shares(count, total, most, skew, full):
    portions = [(1 << 20) // math.isqrt(standing ** skew) + 1 for standing in range(1, count + 1)]
    largest = most if full else min(most, max(-(-total // count), total * portions[0] // sum(portions)))
    least = 1 if total - largest >= count - 1 else 0
    holding, spare = [largest] + [least] * (count - 1), total - largest - least * (count - 1)
    while spare > 0:
        free = [i for i in range(1, count) if holding[i] < largest] or [i for i in range(1, count) if holding[i] < most]
        mass, budget = sum([portions[i] for i in free]), spare
        for i in free:
            more = min(most - holding[i], max(1, budget * portions[i] // mass), spare)
            holding[i] = holding[i] + more
            spare = spare - more
    return np.array(holding)


def normal_values(key, shape, deviation, reach, cuts=(), kind=jnp.bfloat16):
    values = deviation * jax.random.normal(key, shape, jnp.float32)
    if cuts:
        values = values * levels(key, shape, cuts, -0.22, 0.18)
    return jnp.clip(values, -reach, reach).astype(kind)


def setup_inputs(seed: int = 0) -> dict:
    seeds = jax.random.split(jax.random.key(seed), 12)
    table_window = normal_values(seeds[0], (WINDOW, D_EMB), 0.5, 3.0, ((0, 8),))
    dense_part = normal_values(seeds[1], (BATCH, D_EMB), 1.0, 6.0, ((0, 32),))
    bag_rows = set_ends(jax.random.randint(seeds[2], (BATCH, TABLES, HOT), 0, LOCAL_ROWS), jax.random.fold_in(seeds[2], 1), 0, LOCAL_ROWS - 1).astype(jnp.int32)
    bag_lengths = set_ends(jax.random.randint(seeds[3], (BATCH, TABLES), 1, HOT + 1), jax.random.fold_in(seeds[3], 1), 1, HOT).astype(jnp.int32)
    bag_owner_keys = jax.random.split(jax.random.fold_in(seeds[4], 1), BATCH * TABLES // (SAMP * TABLES))
    bag_owner_turns = jax.random.permutation(jax.random.fold_in(seeds[4], 3), BATCH * TABLES // (SAMP * TABLES))
    bag_owner = jax.vmap(lambda own, number: routed_block(jax.random.fold_in(seeds[4], 2), own, number, SAMP * TABLES, N_EMB, 1, CAP, 2))(bag_owner_keys, bag_owner_turns).reshape((BATCH, TABLES, 1))
    labels = set_ends((jax.random.randint(seeds[5], (BATCH,), 0, 4) < 1).astype(jnp.int32), jax.random.fold_in(seeds[5], 1), 0, 1)
    sample_weight = draw_sample_weight(jax.random.fold_in(seeds[11], 71), 0)
    down_w = normal_values(seeds[7], (CROSS, RANK), CROSS ** -0.5, 0.109375)
    up_w = normal_values(seeds[8], (RANK, CROSS), RANK ** -0.5, 0.25)
    cross_bias = normal_values(seeds[9], (CROSS,), 0.5, 3.0, (), jnp.float32)
    head_w = normal_values(seeds[10], (CROSS,), CROSS ** -0.5, 0.109375, (), jnp.float32)
    return {"table_window": table_window, "dense_part": dense_part, "bag_rows": bag_rows, "bag_lengths": bag_lengths, "bag_owner": bag_owner, "labels": labels, "sample_weight": sample_weight, "down_w": down_w, "up_w": up_w, "cross_bias": cross_bias, "head_w": head_w}


def reference(table_window, dense_part, bag_rows, bag_lengths, bag_owner, labels, sample_weight, down_w, up_w, cross_bias, head_w):
    block = SAMP * 8
    blocks = BATCH // block
    hot_pos = jnp.arange(HOT, dtype=jnp.int32)

    def step(carry, index):
        row_acc, head_acc, bias_acc = carry
        start = (index * block).astype(jnp.int32)
        rows = lax.dynamic_slice_in_dim(bag_rows, start, block, 0)
        lens = lax.dynamic_slice_in_dim(bag_lengths, start, block, 0)
        owner = lax.dynamic_slice_in_dim(bag_owner, start, block, 0)
        dense = lax.dynamic_slice_in_dim(dense_part, start, block, 0)
        label = lax.dynamic_slice_in_dim(labels, start, block, 0)
        weight = lax.dynamic_slice_in_dim(sample_weight, start, block, 0)
        place = owner[:, :, 0][:, :, None] * LOCAL_ROWS + rows
        live = hot_pos[None, None, :] < lens[:, :, None]
        safe = jnp.where(live, place, 0).astype(jnp.int32)
        gathered = table_window[safe].astype(jnp.float32) * live[..., None].astype(jnp.float32)
        pooled = jnp.sum(gathered, axis=2).astype(jnp.bfloat16).reshape(block, TABLES * D_EMB)
        x0 = jnp.concatenate([dense, pooled], axis=1)
        low = jnp.dot(x0, down_w, preferred_element_type=jnp.float32).astype(jnp.bfloat16)
        cross = jnp.dot(low, up_w, preferred_element_type=jnp.float32) + cross_bias[None, :]
        x0f = x0.astype(jnp.float32)
        x1 = x0f * cross + x0f
        logit = jnp.dot(x1, head_w, precision=lax.Precision.HIGHEST)
        dlogit = weight * (jax.nn.sigmoid(logit) - label.astype(jnp.float32))
        d_x1 = dlogit[:, None] * head_w[None, :]
        head_acc = head_acc + jnp.dot(dlogit, x1, precision=lax.Precision.HIGHEST)
        bias_acc = bias_acc + jnp.sum(d_x1 * x0f, axis=0)
        d_cross = (d_x1 * x0f).astype(jnp.bfloat16)
        d_low = jnp.dot(d_cross, up_w.T, preferred_element_type=jnp.float32).astype(jnp.bfloat16)
        d_x0 = d_x1 * (cross + 1.0) + jnp.dot(d_low, down_w.T, preferred_element_type=jnp.float32)
        d_pooled = d_x0[:, D_EMB:].astype(jnp.bfloat16).reshape(block, TABLES, D_EMB)
        contrib = d_pooled.astype(jnp.float32)[:, :, None, :] * live[..., None].astype(jnp.float32)
        row_acc = row_acc.at[safe.reshape(-1)].add(contrib.reshape(-1, D_EMB))
        return (row_acc, head_acc, bias_acc), d_x0[:, :D_EMB].astype(jnp.bfloat16)

    init = (jnp.zeros((WINDOW, D_EMB), jnp.float32), jnp.zeros((CROSS,), jnp.float32), jnp.zeros((CROSS,), jnp.float32))
    (row_grad, head_grad, bias_grad), dense_blocks = lax.scan(step, init, jnp.arange(blocks, dtype=jnp.int32))
    return row_grad, head_grad, bias_grad, dense_blocks.reshape(BATCH, D_EMB)
```

```python
import functools

import jax
import jax.numpy as jnp
from jax import lax
from jax.experimental import pallas as pl
from jax.experimental.pallas import tpu as pltpu
from jax.sharding import PartitionSpec as P

BF16 = jnp.bfloat16
F32 = jnp.float32
LANES = 128
CHUNK = 32
VMEM_BYTES = 16 * 1024 * 1024


def params():
    return pltpu.CompilerParams(vmem_limit_bytes=VMEM_BYTES)


VMEM = pl.BlockSpec(memory_space=pltpu.VMEM)


def cost(flops, moved):
    return pl.CostEstimate(flops=flops, bytes_accessed=moved, transcendentals=0)


def ring_place(owner):
    return jnp.where(owner % 2 == 1, owner // 2, 7 - owner // 2)


def diagonal():
    return lax.broadcasted_iota(jnp.int32, (LANES, LANES), 0) == lax.broadcasted_iota(
        jnp.int32, (LANES, LANES), 1
    )


def count_kernel(owners, local_rows, where_ref, place_ref, counts_ref, turn_ref, column_ref):
    tables, hot, _ = place_ref.shape
    rows = counts_ref.shape[0]
    high = rows // LANES
    half, index = where_ref[0], where_ref[1]
    shift = local_rows.bit_length() - 1
    eye = diagonal()
    ones = jnp.ones((LANES, LANES), BF16)
    ids = lax.broadcasted_iota(jnp.int32, (LANES, LANES), 0)

    def table(at, carry):
        place = place_ref[at]
        owner = place[0:1, :] >> shift
        if owners == 8:
            turn = (ring_place(owner) - ring_place(index) + owners) & (owners - 1)
        else:
            turn = owner
        turn = turn.astype(F32)
        turn_ref[pl.ds(at, 1), :] = turn
        lanes = pl.ds(pl.multiple_of(at * LANES, LANES), LANES)
        column_ref[lanes, :] = jnp.dot(
            jnp.where(eye, turn, 0.0).astype(BF16), ones, preferred_element_type=F32
        ).astype(BF16)
        here = (place & (local_rows - 1)) - half * rows
        inside = (place >= 0) & (here >= 0) & (here < rows)
        low = jnp.where(inside, here & (LANES - 1), -1)
        code = jnp.where(inside, jnp.left_shift(1, 4 * (here >> (LANES.bit_length() - 1))), 0)
        for first in range(0, LANES, CHUNK):
            total = 0
            for h in range(hot):
                total = total + jnp.where(
                    ids[first : first + CHUNK] == low[h : h + 1, :], code[h : h + 1, :], 0
                )
            for part in range(high):
                count = lax.shift_right_logical(total, 4 * part) & 15
                start = part * LANES + first
                counts_ref[start : start + CHUNK, lanes] = count.astype(F32).astype(BF16)
        return carry

    lax.fori_loop(0, tables, table, 0, unroll=2)


def bag_counts(where, place, owners, local_rows):
    tables, hot, samples = place.shape
    bags = tables * samples
    rows = local_rows // 2
    return pl.pallas_call(
        functools.partial(count_kernel, owners, local_rows),
        out_shape=(
            jax.ShapeDtypeStruct((rows, bags), BF16),
            jax.ShapeDtypeStruct((tables, samples), F32),
            jax.ShapeDtypeStruct((bags, LANES), BF16),
        ),
        in_specs=[pl.BlockSpec(memory_space=pltpu.SMEM), VMEM],
        out_specs=(VMEM, VMEM, VMEM),
        compiler_params=params(),
        cost_estimate=cost(5 * 10**9, 0),
        name="bag_counts",
    )(where, place)


def pool_kernel(shards, turns, tables, added, turn_ref, counts_ref, *refs):
    sum_ref = refs[-1]
    blocks = refs[: sum(shards)]
    before = refs[sum(shards) : sum(shards) + added]
    left, at = [], 0
    for parts in shards:
        tiles = [
            ref[row : row + LANES, :]
            for ref in blocks[at : at + parts]
            for row in range(0, ref.shape[0], LANES)
        ]
        left.append(jnp.concatenate(tiles, axis=1))
        at += parts
    left = jnp.concatenate(left, axis=0)
    for start in range(0, turn_ref.shape[0], tables):
        bags = slice(start * LANES, (start + tables) * LANES)
        product = jnp.dot(left, counts_ref[:, bags], preferred_element_type=F32)
        for table in range(tables):
            turn = turn_ref[start + table : start + table + 1, :]
            here = slice((start + table) * LANES, (start + table + 1) * LANES)
            total = before[0][:, here] if before else 0.0
            for i, one in enumerate(turns):
                mine = product[i * LANES : (i + 1) * LANES, table * LANES : (table + 1) * LANES]
                total = jnp.where(turn == one, mine, total)
            sum_ref[:, here] = total


def pool(turns, turn, counts, shards, before, ahead=()):
    rows, bags = counts.shape
    blocks = [block for shard in shards for block in shard]
    width = blocks[0].shape[1]
    tables = turn.shape[0]
    extra = ([] if before is None else [before]) + list(ahead)
    return pl.pallas_call(
        functools.partial(
            pool_kernel,
            [len(shard) for shard in shards],
            turns,
            tables if len(turns) <= 4 else tables // 2,
            0 if before is None else 1,
        ),
        out_shape=jax.ShapeDtypeStruct((width, bags), F32),
        in_specs=[VMEM] * (2 + len(blocks) + len(extra)),
        out_specs=VMEM,
        compiler_params=params(),
        cost_estimate=cost(0, 0),
        name="pool",
    )(turn, counts, *blocks, *extra)


def cross_kernel(
    tables,
    dense_ref,
    own_ref,
    other_ref,
    label_ref,
    weight_ref,
    down_ref,
    up_ref,
    bias_ref,
    head_ref,
    d_pooled_ref,
    dense_grad_ref,
    grads_ref,
    x0_ref,
    cross_ref,
    d_cross_ref,
):
    samples = dense_ref.shape[0]
    blocks = tables + 1
    eye = diagonal()
    column = lambda ref: jnp.sum(jnp.where(eye, ref[...], 0.0), axis=1, keepdims=True)
    x0_ref[:, :LANES] = dense_ref[...]
    for table in range(tables):
        here = slice(table * LANES, (table + 1) * LANES)
        x0_ref[:, (table + 1) * LANES : (table + 2) * LANES] = (
            (own_ref[:, here] + other_ref[:, here]).T.astype(BF16)
        )
    low = jnp.dot(x0_ref[...], down_ref[...], preferred_element_type=F32).astype(BF16)
    logit = jnp.zeros((samples, LANES), F32)
    for block in range(blocks):
        here = slice(block * LANES, (block + 1) * LANES)
        cross = jnp.dot(low, up_ref[:, here], preferred_element_type=F32) + bias_ref[block : block + 1, :]
        cross_ref[:, here] = cross
        x0f = x0_ref[:, here].astype(F32)
        logit = logit + (x0f * cross + x0f) * head_ref[block : block + 1, :]
    logit = jnp.sum(logit, axis=1, keepdims=True)
    d_logit = column(weight_ref) * (jax.nn.sigmoid(logit) - column(label_ref))
    for block in range(blocks):
        here = slice(block * LANES, (block + 1) * LANES)
        x0f = x0_ref[:, here].astype(F32)
        x1 = x0f * cross_ref[:, here] + x0f
        grads_ref[0, block : block + 1, :] = jnp.sum(d_logit * x1, axis=0, keepdims=True)
        d_cross = d_logit * head_ref[block : block + 1, :] * x0f
        grads_ref[1, block : block + 1, :] = jnp.sum(d_cross, axis=0, keepdims=True)
        d_cross_ref[:, here] = d_cross.astype(BF16)
    d_low = lax.dot_general(
        d_cross_ref[...], up_ref[...], (((1,), (1,)), ((), ())), preferred_element_type=F32
    ).astype(BF16)
    for block in range(blocks):
        here = slice(block * LANES, (block + 1) * LANES)
        d_x1 = d_logit * head_ref[block : block + 1, :]
        d_x0 = d_x1 * (cross_ref[:, here] + 1.0) + lax.dot_general(
            d_low, down_ref[here, :], (((1,), (1,)), ((), ())), preferred_element_type=F32
        )
        if block == 0:
            dense_grad_ref[...] = d_x0.astype(BF16)
        else:
            place = slice((block - 1) * samples, block * samples)
            d_pooled_ref[place, :] = d_x0.astype(BF16)


def cross_layer(dense, own, other, labels, weights, down_w, up_w, bias, head):
    samples, width = dense.shape
    tables = own.shape[1] // samples
    cross = down_w.shape[0]
    return pl.pallas_call(
        functools.partial(cross_kernel, tables),
        out_shape=(
            jax.ShapeDtypeStruct((tables * samples, width), BF16),
            jax.ShapeDtypeStruct((samples, width), BF16),
            jax.ShapeDtypeStruct((2, cross // LANES, LANES), F32),
        ),
        scratch_shapes=[
            pltpu.VMEM((samples, cross), BF16),
            pltpu.VMEM((samples, cross), F32),
            pltpu.VMEM((samples, cross), BF16),
        ],
        compiler_params=params(),
        cost_estimate=cost(8 * 10**9, 12 * 10**6),
        name="cross_layer",
    )(dense, own, other, labels, weights, down_w, up_w, bias, head)


def spread_kernel(turns, count, at, *refs):
    sides = [refs[3 * i : 3 * i + 3] for i in range(count)]
    before = refs[3 * count : -1 - count]
    rows_ref, masked = refs[-1 - count], refs[-count:]
    zero = jnp.array(0, BF16)
    for (column_ref, gradient_ref, _), masked_ref in zip(sides, masked):
        for i, one in enumerate(turns):
            masked_ref[:, i * LANES : (i + 1) * LANES] = jnp.where(
                column_ref[...] == jnp.array(one, BF16), gradient_ref[...], zero
            )
    total = before[0][:, at * LANES : (at + len(turns)) * LANES] if before else None
    for (_, _, counts_ref), masked_ref in zip(sides, masked):
        part = jnp.dot(counts_ref[...], masked_ref[...], preferred_element_type=F32)
        total = part if total is None else total + part
    rows_ref[...] = total


def spread(turns, sides, before=None, at=0):
    bags, width = sides[0][1].shape
    rows = sides[0][2].shape[0]
    wide = len(turns) * width
    operands = [one for side in sides for one in side] + ([] if before is None else [before])
    return pl.pallas_call(
        functools.partial(spread_kernel, turns, len(sides), at),
        out_shape=jax.ShapeDtypeStruct((rows, wide), F32),
        in_specs=[VMEM] * len(operands),
        out_specs=VMEM,
        scratch_shapes=[pltpu.VMEM((bags, wide), BF16)] * len(sides),
        compiler_params=params(),
        cost_estimate=cost(0, 0),
        name="spread",
    )(*operands)


def place_kernel(at_ref, part_ref, *refs):
    rows_ref, sem = refs[-2], refs[-1]
    rows = part_ref.shape[0]
    start = pl.multiple_of(at_ref[0] * rows, rows)
    copy = pltpu.make_async_copy(part_ref, rows_ref.at[pl.ds(start, rows), :], sem)
    copy.start()
    copy.wait()


def place_half(at, part, before=None):
    rows, width = part.shape
    either = pl.BlockSpec(memory_space=pl.ANY)
    return pl.pallas_call(
        place_kernel,
        out_shape=jax.ShapeDtypeStruct((2 * rows, width), F32),
        in_specs=[pl.BlockSpec(memory_space=pltpu.SMEM), VMEM] + [either] * (before is not None),
        out_specs=either,
        scratch_shapes=[pltpu.SemaphoreType.DMA],
        input_output_aliases={} if before is None else {2: 0},
        compiler_params=params(),
        cost_estimate=cost(0, 0),
        name="place_half",
    )(at, part, *([] if before is None else [before]))


def swap(value, axis, stride):
    size = lax.axis_size(axis)
    return lax.ppermute(value, axis, [(i, i ^ stride) for i in range(size)])


def sum_pairs(value, axis, stride, wire):
    while stride < lax.axis_size(axis):
        value = value.astype(wire)
        value = value.astype(F32) + swap(value, axis, stride).astype(F32)
        stride *= 2
    return value


def ring_order(size):
    inner = 1 << ((size.bit_length() - 1) // 2)
    outer = size // inner
    cycle = []
    for far in range(outer):
        columns = range(1, inner) if far % 2 == 0 else range(inner - 1, 0, -1)
        cycle += [far * inner + column for column in columns]
    return cycle + [far * inner for far in range(outer - 1, -1, -1)]


def ring_turns(owners):
    order = ring_order(owners)
    right = [(order[i], order[(i + 1) % owners]) for i in range(owners)]
    return right, [(there, here) for here, there in right]


def count_and_pool(where, place, shard, local_rows, ahead):
    owners = lax.axis_size("emb")
    count = lambda own: bag_counts(where, own, owners, local_rows)
    places = [place, swap(place, "grp", 1)]
    sums = [None, None]

    def add(side, turns, shards, ahead=()):
        sums[side] = pool(turns, sides[side][1], sides[side][0], shards, sums[side], ahead)

    if owners != 8:
        sides = [count(one) for one in places]
        table = lax.all_gather(shard, "emb", axis=0, tiled=False)
        for start in range(0, owners, 8):
            here = tuple(range(start, start + 8))
            for side in (1, 0):
                add(side, here, [[table[one]] for one in here])
        return sides, sums
    right, left = ring_turns(owners)
    lefts, rights = [shard], [shard]

    def step(beside):
        before = lefts[-1], rights[-1], beside
        a, b, beside = before if beside is None else lax.optimization_barrier(before)
        lefts.append(lax.ppermute(a, "emb", right))
        rights.append(lax.ppermute(b, "emb", left))
        return beside

    step(None)
    own, places[1] = step((count(places[0]), places[1]))
    sides = list(step([own, count(places[1])]))
    near = (0, 1, 7), [[shard], [rights[1]], [lefts[1]]]
    add(1, *near)
    add(1, (2, 6), [[rights[2]], [lefts[2]]], ahead)
    add(0, *near)
    middle = shard.shape[0] // 2
    a, b, sums[0], sums[1] = lax.optimization_barrier(
        (lefts[3][:middle], rights[3][middle:], sums[0], sums[1])
    )
    far = [lax.ppermute(a, "emb", right), lax.ppermute(b, "emb", left)]
    add(0, (2, 6), [[rights[2]], [lefts[2]]])
    add(1, (3, 5), [[rights[3]], [lefts[3]]])
    add(1, (4,), [far])
    sums[0], sums[1] = lax.optimization_barrier((sums[0], sums[1]))
    add(0, (3, 5), [[rights[3]], [lefts[3]]])
    add(0, (4,), [far])
    return sides, sums


def spread_and_sum(sides, grads):
    owners = lax.axis_size("emb")
    width = sides[0][1].shape[1]
    exchanges = [
        (axis, 1 << bit)
        for axis in ("grp", "emb")
        for bit in range(lax.axis_size(axis).bit_length() - 1)
    ][1:]
    if owners != 8 or len(exchanges) != 4:
        parts = [
            spread(tuple(range(start, start + 4)), sides).astype(BF16)
            for start in range(0, owners, 4)
        ]
        for axis, stride in exchanges:
            grads = grads + swap(grads, axis, stride)
        part = lax.psum_scatter(
            jnp.concatenate(parts, axis=1), "emb", scatter_dimension=1, tiled=True
        )
        return sum_pairs(part, "grp", 2, BF16), grads
    right, left = ring_turns(owners)

    def exchange(grads):
        return grads + swap(grads, *exchanges.pop(0))

    def send(to_right, to_left):
        return lax.ppermute(to_right, "emb", right), lax.ppermute(to_left, "emb", left)

    def messages(part, went_right, went_left):
        to_right, to_left = part[:, :width], part[:, width:]
        return (to_right + went_right).astype(BF16), (to_left + went_left).astype(BF16)

    own = spread((4, 0), sides[:1])
    part = spread((4, 0), sides[1:], own)
    far, mine = part[:, :width].astype(BF16), part[:, width:]
    middle = far.shape[0] // 2
    far, sides, grads = lax.optimization_barrier((far, sides, grads))
    went_right, went_left = send(far[:middle], far[middle:])
    went_right = jnp.pad(went_right.astype(F32), ((0, middle), (0, 0)))
    went_left = jnp.pad(went_left.astype(F32), ((middle, 0), (0, 0)))
    for step in (3, 2, 1):
        part = spread((step, owners - step), sides)
        to_right, to_left = messages(part, went_right, went_left)
        to_right, to_left, sides, grads = lax.optimization_barrier((to_right, to_left, sides, grads))
        went_right, went_left = send(to_right, to_left)
        grads = exchange(grads)
        went_right, went_left = went_right.astype(F32), went_left.astype(F32)
    total = (mine + went_right + went_left).astype(BF16)
    total, grads = lax.optimization_barrier((total, grads))
    other, grads = lax.optimization_barrier((swap(total, "grp", 2), exchange(grads)))
    return total.astype(F32) + other.astype(F32), grads


def body(
    table_window,
    dense_part,
    bag_rows,
    bag_lengths,
    bag_owner,
    labels,
    sample_weight,
    down_w,
    up_w,
    cross_bias,
    head_w,
):
    samples, tables, hot = bag_rows.shape
    local_rows, width = table_window.shape
    rows = local_rows // 2
    half = (lax.axis_index("grp") % 2).astype(jnp.int32)
    where = jnp.stack([half, lax.axis_index("emb").astype(jnp.int32)])
    shard = lax.dynamic_slice_in_dim(table_window, half * rows, rows, 0)
    shard = shard.reshape(-1, LANES, width).transpose(0, 2, 1).reshape(rows, LANES)
    live = jnp.arange(hot, dtype=jnp.int32)[None, :, None] < bag_lengths.T[:, None, :]
    place = bag_owner.transpose(1, 2, 0) * local_rows + bag_rows.transpose(1, 2, 0)
    place = jnp.where(live, place, -1)
    sides, (own, lent) = count_and_pool(where, place, shard, local_rows, (down_w, up_w))
    other = swap(lent, "grp", 1)
    d_pooled, dense_grad, grads = cross_layer(
        dense_part,
        own,
        other,
        labels.astype(F32).reshape(1, samples),
        sample_weight.reshape(1, samples),
        down_w,
        up_w,
        cross_bias.reshape(-1, LANES),
        head_w.reshape(-1, LANES),
    )
    grads = grads + swap(grads, "grp", 1)
    sides = [
        (sides[0][2], d_pooled, sides[0][0]),
        (sides[1][2], swap(d_pooled, "grp", 1), sides[1][0]),
    ]
    row_half, grads = spread_and_sum(sides, grads)
    at = half.reshape(1)
    row_grad = place_half(1 - at, swap(row_half, "grp", 1), place_half(at, row_half))
    return (row_grad, grads[0].reshape(-1), grads[1].reshape(-1), dense_grad)


def solution(mesh):
    in_specs = (
        P("emb", None),
        P(("grp", "emb"), None),
        P(("grp", "emb"), None, None),
        P(("grp", "emb"), None),
        P(("grp", "emb"), None, None),
        P(("grp", "emb")),
        P(("grp", "emb")),
        P(),
        P(),
        P(),
        P(),
    )
    out_specs = (P("emb", None), P(), P(), P(("grp", "emb"), None))
    return jax.shard_map(body, mesh=mesh, in_specs=in_specs, out_specs=out_specs, check_vma=False)
```

```python
import functools

import jax
import jax.numpy as jnp
from jax import lax
from jax.experimental import pallas as pl
from jax.experimental.pallas import tpu as pltpu
from jax.sharding import PartitionSpec as P

BF16 = jnp.bfloat16
F32 = jnp.float32
LANES = 128
CHUNK = 32
VMEM_BYTES = 16 * 1024 * 1024


def params():
    return pltpu.CompilerParams(vmem_limit_bytes=VMEM_BYTES)


VMEM = pl.BlockSpec(memory_space=pltpu.VMEM)


def cost(flops, moved):
    return pl.CostEstimate(flops=flops, bytes_accessed=moved, transcendentals=0)


def ring_place(owner):
    return jnp.where(owner % 2 == 1, owner // 2, 7 - owner // 2)


def diagonal():
    return lax.broadcasted_iota(jnp.int32, (LANES, LANES), 0) == lax.broadcasted_iota(
        jnp.int32, (LANES, LANES), 1
    )


def side_by_side(blocks):
    tiles = [ref[row : row + LANES, :] for ref in blocks for row in range(0, ref.shape[0], LANES)]
    return jnp.concatenate(tiles, axis=1)


def count_kernel(owners, local_rows, turns, where_ref, place_ref, *refs):
    if turns:
        counts_ref, turn_ref, column_ref, sum_ref = refs[-4:]
        own_turn_ref, own_counts_ref, blocks = refs[0], refs[1], refs[2:-4]
    else:
        counts_ref, turn_ref, column_ref = refs
    tables, hot, _ = place_ref.shape
    rows = counts_ref.shape[0]
    high = rows // LANES
    half, index = where_ref[0], where_ref[1]
    shift = local_rows.bit_length() - 1
    eye = diagonal()
    ones = jnp.ones((LANES, LANES), BF16)
    ids = lax.broadcasted_iota(jnp.int32, (LANES, LANES), 0)

    def table(at, carry):
        place = place_ref[at]
        owner = place[0:1, :] >> shift
        if owners == 8:
            turn = (ring_place(owner) - ring_place(index) + owners) & (owners - 1)
        else:
            turn = owner
        turn = turn.astype(F32)
        turn_ref[pl.ds(at, 1), :] = turn
        lanes = pl.ds(pl.multiple_of(at * LANES, LANES), LANES)
        column_ref[lanes, :] = jnp.dot(
            jnp.where(eye, turn, 0.0).astype(BF16), ones, preferred_element_type=F32
        ).astype(BF16)
        here = (place & (local_rows - 1)) - half * rows
        inside = (place >= 0) & (here >= 0) & (here < rows)
        low = jnp.where(inside, here & (LANES - 1), -1)
        code = jnp.where(inside, jnp.left_shift(1, 4 * (here >> (LANES.bit_length() - 1))), 0)
        for first in range(0, LANES, CHUNK):
            total = 0
            for h in range(hot):
                total = total + jnp.where(
                    ids[first : first + CHUNK] == low[h : h + 1, :], code[h : h + 1, :], 0
                )
            for part in range(high):
                count = lax.shift_right_logical(total, 4 * part) & 15
                start = part * LANES + first
                counts_ref[start : start + CHUNK, lanes] = count.astype(F32).astype(BF16)
        return carry

    def pair(at, carry):
        lanes = pl.ds(pl.multiple_of(at * 2 * LANES, 2 * LANES), 2 * LANES)
        left = jnp.concatenate([side_by_side([block]) for block in blocks], axis=0)
        product = jnp.dot(left, own_counts_ref[:, lanes], preferred_element_type=F32)
        for one in range(2):
            table(2 * at + one, 0)
        total = []
        for one in range(2):
            turn = own_turn_ref[pl.ds(2 * at + one, 1), :]
            part = 0.0
            for i, each in enumerate(turns):
                mine = product[i * LANES : (i + 1) * LANES, one * LANES : (one + 1) * LANES]
                part = jnp.where(turn == each, mine, part)
            total.append(part)
        sum_ref[:, lanes] = jnp.concatenate(total, axis=1)
        return carry

    if turns:
        lax.fori_loop(0, tables // 2, pair, 0)
    else:
        lax.fori_loop(0, tables, table, 0, unroll=2)


def bag_counts(where, place, owners, local_rows, turns=(), own=(), shards=()):
    tables, hot, samples = place.shape
    bags = tables * samples
    rows = local_rows // 2
    operands = [*own, *shards] if turns else []
    out_shape = (
        jax.ShapeDtypeStruct((rows, bags), BF16),
        jax.ShapeDtypeStruct((tables, samples), F32),
        jax.ShapeDtypeStruct((bags, LANES), BF16),
    ) + ((jax.ShapeDtypeStruct((LANES, bags), F32),) if turns else ())
    return pl.pallas_call(
        functools.partial(count_kernel, owners, local_rows, turns),
        out_shape=out_shape,
        in_specs=[pl.BlockSpec(memory_space=pltpu.SMEM)] + [VMEM] * (1 + len(operands)),
        out_specs=(VMEM,) * len(out_shape),
        compiler_params=params(),
        cost_estimate=cost(5 * 10**9, 0),
        name="bag_counts",
    )(where, place, *operands)


def pool_kernel(shards, turns, tables, added, turn_ref, counts_ref, *refs):
    sum_ref = refs[-1]
    blocks = refs[: sum(shards)]
    before = refs[sum(shards) : sum(shards) + added]
    left, at = [], 0
    for parts in shards:
        left.append(side_by_side(blocks[at : at + parts]))
        at += parts
    left = jnp.concatenate(left, axis=0)
    for start in range(0, turn_ref.shape[0], tables):
        bags = slice(start * LANES, (start + tables) * LANES)
        product = jnp.dot(left, counts_ref[:, bags], preferred_element_type=F32)
        for table in range(tables):
            turn = turn_ref[start + table : start + table + 1, :]
            here = slice((start + table) * LANES, (start + table + 1) * LANES)
            total = before[0][:, here] if before else 0.0
            for i, one in enumerate(turns):
                mine = product[i * LANES : (i + 1) * LANES, table * LANES : (table + 1) * LANES]
                total = jnp.where(turn == one, mine, total)
            sum_ref[:, here] = total


def pool(turns, turn, counts, shards, before, ahead=()):
    rows, bags = counts.shape
    blocks = [block for shard in shards for block in shard]
    width = blocks[0].shape[1]
    tables = turn.shape[0]
    extra = ([] if before is None else [before]) + list(ahead)
    return pl.pallas_call(
        functools.partial(
            pool_kernel,
            [len(shard) for shard in shards],
            turns,
            tables if len(turns) <= 4 else tables // 2,
            0 if before is None else 1,
        ),
        out_shape=jax.ShapeDtypeStruct((width, bags), F32),
        in_specs=[VMEM] * (2 + len(blocks) + len(extra)),
        out_specs=VMEM,
        compiler_params=params(),
        cost_estimate=cost(0, 0),
        name="pool",
    )(turn, counts, *blocks, *extra)


def cross_kernel(
    tables,
    dense_ref,
    own_ref,
    other_ref,
    label_ref,
    weight_ref,
    down_ref,
    up_ref,
    bias_ref,
    head_ref,
    d_pooled_ref,
    dense_grad_ref,
    grads_ref,
    x0_ref,
    cross_ref,
    d_cross_ref,
):
    samples = dense_ref.shape[0]
    blocks = tables + 1
    eye = diagonal()
    column = lambda ref: jnp.sum(jnp.where(eye, ref[...], 0.0), axis=1, keepdims=True)
    x0_ref[:, :LANES] = dense_ref[...]
    for table in range(tables):
        here = slice(table * LANES, (table + 1) * LANES)
        x0_ref[:, (table + 1) * LANES : (table + 2) * LANES] = (
            (own_ref[:, here] + other_ref[:, here]).T.astype(BF16)
        )
    low = jnp.dot(x0_ref[...], down_ref[...], preferred_element_type=F32).astype(BF16)
    logit = jnp.zeros((samples, LANES), F32)
    for block in range(blocks):
        here = slice(block * LANES, (block + 1) * LANES)
        cross = jnp.dot(low, up_ref[:, here], preferred_element_type=F32) + bias_ref[block : block + 1, :]
        cross_ref[:, here] = cross
        x0f = x0_ref[:, here].astype(F32)
        logit = logit + (x0f * cross + x0f) * head_ref[block : block + 1, :]
    logit = jnp.sum(logit, axis=1, keepdims=True)
    d_logit = column(weight_ref) * (jax.nn.sigmoid(logit) - column(label_ref))
    for block in range(blocks):
        here = slice(block * LANES, (block + 1) * LANES)
        x0f = x0_ref[:, here].astype(F32)
        x1 = x0f * cross_ref[:, here] + x0f
        grads_ref[0, block : block + 1, :] = jnp.sum(d_logit * x1, axis=0, keepdims=True)
        d_cross = d_logit * head_ref[block : block + 1, :] * x0f
        grads_ref[1, block : block + 1, :] = jnp.sum(d_cross, axis=0, keepdims=True)
        d_cross_ref[:, here] = d_cross.astype(BF16)
    d_low = lax.dot_general(
        d_cross_ref[...], up_ref[...], (((1,), (1,)), ((), ())), preferred_element_type=F32
    ).astype(BF16)
    for block in range(blocks):
        here = slice(block * LANES, (block + 1) * LANES)
        d_x1 = d_logit * head_ref[block : block + 1, :]
        d_x0 = d_x1 * (cross_ref[:, here] + 1.0) + lax.dot_general(
            d_low, down_ref[here, :], (((1,), (1,)), ((), ())), preferred_element_type=F32
        )
        if block == 0:
            dense_grad_ref[...] = d_x0.astype(BF16)
        else:
            place = slice((block - 1) * samples, block * samples)
            d_pooled_ref[place, :] = d_x0.astype(BF16)


def cross_layer(dense, own, other, labels, weights, down_w, up_w, bias, head):
    samples, width = dense.shape
    tables = own.shape[1] // samples
    cross = down_w.shape[0]
    return pl.pallas_call(
        functools.partial(cross_kernel, tables),
        out_shape=(
            jax.ShapeDtypeStruct((tables * samples, width), BF16),
            jax.ShapeDtypeStruct((samples, width), BF16),
            jax.ShapeDtypeStruct((2, cross // LANES, LANES), F32),
        ),
        scratch_shapes=[
            pltpu.VMEM((samples, cross), BF16),
            pltpu.VMEM((samples, cross), F32),
            pltpu.VMEM((samples, cross), BF16),
        ],
        compiler_params=params(),
        cost_estimate=cost(8 * 10**9, 12 * 10**6),
        name="cross_layer",
    )(dense, own, other, labels, weights, down_w, up_w, bias, head)


def spread_kernel(turns, count, at, *refs):
    sides = [refs[3 * i : 3 * i + 3] for i in range(count)]
    before = refs[3 * count : -1 - count]
    rows_ref, masked = refs[-1 - count], refs[-count:]
    zero = jnp.array(0, BF16)
    for (column_ref, gradient_ref, _), masked_ref in zip(sides, masked):
        for i, one in enumerate(turns):
            masked_ref[:, i * LANES : (i + 1) * LANES] = jnp.where(
                column_ref[...] == jnp.array(one, BF16), gradient_ref[...], zero
            )
    total = before[0][:, at * LANES : (at + len(turns)) * LANES] if before else None
    for (_, _, counts_ref), masked_ref in zip(sides, masked):
        part = jnp.dot(counts_ref[...], masked_ref[...], preferred_element_type=F32)
        total = part if total is None else total + part
    rows_ref[...] = total


def spread(turns, sides, before=None, at=0):
    bags, width = sides[0][1].shape
    rows = sides[0][2].shape[0]
    wide = len(turns) * width
    operands = [one for side in sides for one in side] + ([] if before is None else [before])
    return pl.pallas_call(
        functools.partial(spread_kernel, turns, len(sides), at),
        out_shape=jax.ShapeDtypeStruct((rows, wide), F32),
        in_specs=[VMEM] * len(operands),
        out_specs=VMEM,
        scratch_shapes=[pltpu.VMEM((bags, wide), BF16)] * len(sides),
        compiler_params=params(),
        cost_estimate=cost(0, 0),
        name="spread",
    )(*operands)


def place_kernel(at_ref, part_ref, *refs):
    rows_ref, sem = refs[-2], refs[-1]
    rows = part_ref.shape[0]
    start = pl.multiple_of(at_ref[0] * rows, rows)
    copy = pltpu.make_async_copy(part_ref, rows_ref.at[pl.ds(start, rows), :], sem)
    copy.start()
    copy.wait()


def place_half(at, part, before=None):
    rows, width = part.shape
    either = pl.BlockSpec(memory_space=pl.ANY)
    return pl.pallas_call(
        place_kernel,
        out_shape=jax.ShapeDtypeStruct((2 * rows, width), F32),
        in_specs=[pl.BlockSpec(memory_space=pltpu.SMEM), VMEM] + [either] * (before is not None),
        out_specs=either,
        scratch_shapes=[pltpu.SemaphoreType.DMA],
        input_output_aliases={} if before is None else {2: 0},
        compiler_params=params(),
        cost_estimate=cost(0, 0),
        name="place_half",
    )(at, part, *([] if before is None else [before]))


def swap(value, axis, stride):
    size = lax.axis_size(axis)
    return lax.ppermute(value, axis, [(i, i ^ stride) for i in range(size)])


def sum_pairs(value, axis, stride, wire):
    while stride < lax.axis_size(axis):
        value = value.astype(wire)
        value = value.astype(F32) + swap(value, axis, stride).astype(F32)
        stride *= 2
    return value


def ring_order(size):
    inner = 1 << ((size.bit_length() - 1) // 2)
    outer = size // inner
    cycle = []
    for far in range(outer):
        columns = range(1, inner) if far % 2 == 0 else range(inner - 1, 0, -1)
        cycle += [far * inner + column for column in columns]
    return cycle + [far * inner for far in range(outer - 1, -1, -1)]


def ring_turns(owners):
    order = ring_order(owners)
    right = [(order[i], order[(i + 1) % owners]) for i in range(owners)]
    return right, [(there, here) for here, there in right]


def count_and_pool(where, place, shard, local_rows, ahead):
    owners = lax.axis_size("emb")
    count = lambda own: bag_counts(where, own, owners, local_rows)
    places = [place, swap(place, "grp", 1)]
    sums = [None, None]

    def add(side, turns, shards, ahead=()):
        sums[side] = pool(turns, sides[side][1], sides[side][0], shards, sums[side], ahead)

    if owners != 8:
        sides = [count(one) for one in places]
        table = lax.all_gather(shard, "emb", axis=0, tiled=False)
        for start in range(0, owners, 8):
            here = tuple(range(start, start + 8))
            for side in (1, 0):
                add(side, here, [[table[one]] for one in here])
        return sides, sums
    right, left = ring_turns(owners)
    lefts, rights = [shard], [shard]

    def step(beside):
        before = lefts[-1], rights[-1], beside
        a, b, beside = before if beside is None else lax.optimization_barrier(before)
        lefts.append(lax.ppermute(a, "emb", right))
        rights.append(lax.ppermute(b, "emb", left))
        return beside

    step(None)
    own, places[1] = step((count(places[0]), places[1]))
    near = (0, 1, 7), [[shard], [rights[1]], [lefts[1]]]
    *lent, sums[0] = bag_counts(
        where, places[1], owners, local_rows, near[0], (own[1], own[0]), [one for one, in near[1]]
    )
    *sides, sums[0] = step([own, lent, sums[0]])
    add(1, *near)
    add(1, (2, 6), [[rights[2]], [lefts[2]]], ahead)
    add(0, (2, 6), [[rights[2]], [lefts[2]]])
    middle = shard.shape[0] // 2
    a, b, sums[0], sums[1] = lax.optimization_barrier(
        (lefts[3][:middle], rights[3][middle:], sums[0], sums[1])
    )
    far = [lax.ppermute(a, "emb", right), lax.ppermute(b, "emb", left)]
    for side in (1, 0):
        add(side, (3, 5), [[rights[3]], [lefts[3]]])
    sums[0], sums[1] = lax.optimization_barrier((sums[0], sums[1]))
    for side in (1, 0):
        add(side, (4,), [far])
    return sides, sums


def spread_and_sum(sides, grads):
    owners = lax.axis_size("emb")
    width = sides[0][1].shape[1]
    exchanges = [
        (axis, 1 << bit)
        for axis in ("grp", "emb")
        for bit in range(lax.axis_size(axis).bit_length() - 1)
    ][1:]
    if owners != 8 or len(exchanges) != 4:
        parts = [
            spread(tuple(range(start, start + 4)), sides).astype(BF16)
            for start in range(0, owners, 4)
        ]
        for axis, stride in exchanges:
            grads = grads + swap(grads, axis, stride)
        part = lax.psum_scatter(
            jnp.concatenate(parts, axis=1), "emb", scatter_dimension=1, tiled=True
        )
        return sum_pairs(part, "grp", 2, BF16), grads
    right, left = ring_turns(owners)

    def exchange(grads):
        return grads + swap(grads, *exchanges.pop(0))

    def send(to_right, to_left):
        return lax.ppermute(to_right, "emb", right), lax.ppermute(to_left, "emb", left)

    def messages(part, went_right, went_left):
        to_right, to_left = part[:, :width], part[:, width:]
        return (to_right + went_right).astype(BF16), (to_left + went_left).astype(BF16)

    own = spread((4, 0), sides[:1])
    part = spread((4, 0), sides[1:], own)
    far, mine = part[:, :width].astype(BF16), part[:, width:]
    middle = far.shape[0] // 2
    far, sides, grads = lax.optimization_barrier((far, sides, grads))
    went_right, went_left = send(far[:middle], far[middle:])
    went_right = jnp.pad(went_right.astype(F32), ((0, middle), (0, 0)))
    went_left = jnp.pad(went_left.astype(F32), ((middle, 0), (0, 0)))
    for step in (3, 2, 1):
        part = spread((step, owners - step), sides)
        to_right, to_left = messages(part, went_right, went_left)
        to_right, to_left, sides, grads = lax.optimization_barrier((to_right, to_left, sides, grads))
        went_right, went_left = send(to_right, to_left)
        grads = exchange(grads)
        went_right, went_left = went_right.astype(F32), went_left.astype(F32)
    total = (mine + went_right + went_left).astype(BF16)
    total, grads = lax.optimization_barrier((total, grads))
    other, grads = lax.optimization_barrier((swap(total, "grp", 2), exchange(grads)))
    return total.astype(F32) + other.astype(F32), grads


def body(
    table_window,
    dense_part,
    bag_rows,
    bag_lengths,
    bag_owner,
    labels,
    sample_weight,
    down_w,
    up_w,
    cross_bias,
    head_w,
):
    samples, tables, hot = bag_rows.shape
    local_rows, width = table_window.shape
    rows = local_rows // 2
    half = (lax.axis_index("grp") % 2).astype(jnp.int32)
    where = jnp.stack([half, lax.axis_index("emb").astype(jnp.int32)])
    shard = lax.dynamic_slice_in_dim(table_window, half * rows, rows, 0)
    shard = shard.reshape(-1, LANES, width).transpose(0, 2, 1).reshape(rows, LANES)
    live = jnp.arange(hot, dtype=jnp.int32)[None, :, None] < bag_lengths.T[:, None, :]
    place = bag_owner.transpose(1, 2, 0) * local_rows + bag_rows.transpose(1, 2, 0)
    place = jnp.where(live, place, -1)
    sides, (own, lent) = count_and_pool(where, place, shard, local_rows, (down_w, up_w))
    other = swap(lent, "grp", 1)
    d_pooled, dense_grad, grads = cross_layer(
        dense_part,
        own,
        other,
        labels.astype(F32).reshape(1, samples),
        sample_weight.reshape(1, samples),
        down_w,
        up_w,
        cross_bias.reshape(-1, LANES),
        head_w.reshape(-1, LANES),
    )
    grads = grads + swap(grads, "grp", 1)
    sides = [
        (sides[0][2], d_pooled, sides[0][0]),
        (sides[1][2], swap(d_pooled, "grp", 1), sides[1][0]),
    ]
    row_half, grads = spread_and_sum(sides, grads)
    at = half.reshape(1)
    row_grad = place_half(1 - at, swap(row_half, "grp", 1), place_half(at, row_half))
    return (row_grad, grads[0].reshape(-1), grads[1].reshape(-1), dense_grad)


def solution(mesh):
    in_specs = (
        P("emb", None),
        P(("grp", "emb"), None),
        P(("grp", "emb"), None, None),
        P(("grp", "emb"), None),
        P(("grp", "emb"), None, None),
        P(("grp", "emb")),
        P(("grp", "emb")),
        P(),
        P(),
        P(),
        P(),
    )
    out_specs = (P("emb", None), P(), P(), P(("grp", "emb"), None))
    return jax.shard_map(body, mesh=mesh, in_specs=in_specs, out_specs=out_specs, check_vma=False)
```

```python
import functools

import jax
import jax.numpy as jnp
from jax import lax
from jax.experimental import pallas as pl
from jax.experimental.pallas import tpu as pltpu
from jax.sharding import PartitionSpec as P

BF16 = jnp.bfloat16
F32 = jnp.float32
LANES = 128
CHUNK = 32
VMEM_BYTES = 16 * 1024 * 1024


def params():
    return pltpu.CompilerParams(vmem_limit_bytes=VMEM_BYTES)


VMEM = pl.BlockSpec(memory_space=pltpu.VMEM)


def cost(flops, moved):
    return pl.CostEstimate(flops=flops, bytes_accessed=moved, transcendentals=0)


def ring_place(owner):
    return jnp.where(owner % 2 == 1, owner // 2, 7 - owner // 2)


def diagonal():
    return lax.broadcasted_iota(jnp.int32, (LANES, LANES), 0) == lax.broadcasted_iota(
        jnp.int32, (LANES, LANES), 1
    )


def side_by_side(blocks):
    tiles = [ref[row : row + LANES, :] for ref in blocks for row in range(0, ref.shape[0], LANES)]
    return jnp.concatenate(tiles, axis=1)


def count_kernel(owners, local_rows, turns, where_ref, place_ref, *refs):
    if turns:
        counts_ref, turn_ref, column_ref, sum_ref = refs[-4:]
        own_turn_ref, own_counts_ref, blocks = refs[0], refs[1], refs[2:-4]
    else:
        counts_ref, turn_ref, column_ref = refs
    tables, hot, _ = place_ref.shape
    rows = counts_ref.shape[0]
    high = rows // LANES
    half, index = where_ref[0], where_ref[1]
    shift = local_rows.bit_length() - 1
    eye = diagonal()
    ones = jnp.ones((LANES, LANES), BF16)
    ids = lax.broadcasted_iota(jnp.int32, (LANES, LANES), 0)

    def table(at, carry):
        place = place_ref[at]
        owner = place[0:1, :] >> shift
        if owners == 8:
            turn = (ring_place(owner) - ring_place(index) + owners) & (owners - 1)
        else:
            turn = owner
        turn = turn.astype(F32)
        turn_ref[pl.ds(at, 1), :] = turn
        lanes = pl.ds(pl.multiple_of(at * LANES, LANES), LANES)
        column_ref[lanes, :] = jnp.dot(
            jnp.where(eye, turn, 0.0).astype(BF16), ones, preferred_element_type=F32
        ).astype(BF16)
        here = (place & (local_rows - 1)) - half * rows
        inside = (place >= 0) & (here >= 0) & (here < rows)
        low = jnp.where(inside, here & (LANES - 1), -1)
        code = jnp.where(inside, jnp.left_shift(1, 4 * (here >> (LANES.bit_length() - 1))), 0)
        for first in range(0, LANES, CHUNK):
            total = 0
            for h in range(hot):
                total = total + jnp.where(
                    ids[first : first + CHUNK] == low[h : h + 1, :], code[h : h + 1, :], 0
                )
            for part in range(high):
                count = lax.shift_right_logical(total, 4 * part) & 15
                start = part * LANES + first
                counts_ref[start : start + CHUNK, lanes] = count.astype(F32).astype(BF16)
        return carry

    def pair(at, carry):
        lanes = pl.ds(pl.multiple_of(at * 2 * LANES, 2 * LANES), 2 * LANES)
        left = jnp.concatenate([side_by_side([block]) for block in blocks], axis=0)
        product = jnp.dot(left, own_counts_ref[:, lanes], preferred_element_type=F32)
        for one in range(2):
            table(2 * at + one, 0)
        total = []
        for one in range(2):
            turn = own_turn_ref[pl.ds(2 * at + one, 1), :]
            part = 0.0
            for i, each in enumerate(turns):
                mine = product[i * LANES : (i + 1) * LANES, one * LANES : (one + 1) * LANES]
                part = jnp.where(turn == each, mine, part)
            total.append(part)
        sum_ref[:, lanes] = jnp.concatenate(total, axis=1)
        return carry

    if turns:
        lax.fori_loop(0, tables // 2, pair, 0)
    else:
        lax.fori_loop(0, tables, table, 0, unroll=2)


def bag_counts(where, place, owners, local_rows, turns=(), own=(), shards=()):
    tables, hot, samples = place.shape
    bags = tables * samples
    rows = local_rows // 2
    operands = [*own, *shards] if turns else []
    out_shape = (
        jax.ShapeDtypeStruct((rows, bags), BF16),
        jax.ShapeDtypeStruct((tables, samples), F32),
        jax.ShapeDtypeStruct((bags, LANES), BF16),
    ) + ((jax.ShapeDtypeStruct((LANES, bags), F32),) if turns else ())
    return pl.pallas_call(
        functools.partial(count_kernel, owners, local_rows, turns),
        out_shape=out_shape,
        in_specs=[pl.BlockSpec(memory_space=pltpu.SMEM)] + [VMEM] * (1 + len(operands)),
        out_specs=(VMEM,) * len(out_shape),
        compiler_params=params(),
        cost_estimate=cost(5 * 10**9, 0),
        name="bag_counts",
    )(where, place, *operands)


def pool_kernel(shards, turns, tables, added, turn_ref, counts_ref, *refs):
    sum_ref = refs[-1]
    blocks = refs[: sum(shards)]
    before = refs[sum(shards) : sum(shards) + added]
    left, at = [], 0
    for parts in shards:
        left.append(side_by_side(blocks[at : at + parts]))
        at += parts
    left = jnp.concatenate(left, axis=0)
    for start in range(0, turn_ref.shape[0], tables):
        bags = slice(start * LANES, (start + tables) * LANES)
        product = jnp.dot(left, counts_ref[:, bags], preferred_element_type=F32)
        for table in range(tables):
            turn = turn_ref[start + table : start + table + 1, :]
            here = slice((start + table) * LANES, (start + table + 1) * LANES)
            total = before[0][:, here] if before else jnp.zeros((LANES, LANES), F32)
            for i, one in enumerate(turns):
                mine = product[i * LANES : (i + 1) * LANES, table * LANES : (table + 1) * LANES]
                total = jnp.where(turn == one, mine, total)
            sum_ref[:, here] = total.astype(sum_ref.dtype)


def pool(turns, turn, counts, shards, before, ahead=(), dtype=F32):
    rows, bags = counts.shape
    blocks = [block for shard in shards for block in shard]
    width = blocks[0].shape[1]
    tables = turn.shape[0]
    extra = ([] if before is None else [before]) + list(ahead)
    return pl.pallas_call(
        functools.partial(
            pool_kernel,
            [len(shard) for shard in shards],
            turns,
            tables if len(turns) <= 4 else tables // 2,
            0 if before is None else 1,
        ),
        out_shape=jax.ShapeDtypeStruct((width, bags), dtype),
        in_specs=[VMEM] * (2 + len(blocks) + len(extra)),
        out_specs=VMEM,
        compiler_params=params(),
        cost_estimate=cost(0, 0),
        name="pool",
    )(turn, counts, *blocks, *extra)


def cross_kernel(
    tables,
    dense_ref,
    own_ref,
    other_ref,
    far_ref,
    label_ref,
    weight_ref,
    down_ref,
    up_ref,
    bias_ref,
    head_ref,
    d_pooled_ref,
    dense_grad_ref,
    grads_ref,
    x0_ref,
    cross_ref,
    d_cross_ref,
):
    samples = dense_ref.shape[0]
    blocks = tables + 1
    eye = diagonal()
    column = lambda ref: jnp.sum(jnp.where(eye, ref[...], 0.0), axis=1, keepdims=True)
    x0_ref[:, :LANES] = dense_ref[...]
    for table in range(tables):
        here = slice(table * LANES, (table + 1) * LANES)
        x0_ref[:, (table + 1) * LANES : (table + 2) * LANES] = (
            (own_ref[:, here] + (other_ref[:, here] + far_ref[:, here].astype(F32)))
            .astype(BF16)
            .T
        )
    low = jnp.dot(x0_ref[...], down_ref[...], preferred_element_type=F32).astype(BF16)
    logit = jnp.zeros((samples, LANES), F32)
    for block in range(blocks):
        here = slice(block * LANES, (block + 1) * LANES)
        cross = jnp.dot(low, up_ref[:, here], preferred_element_type=F32) + bias_ref[block : block + 1, :]
        cross_ref[:, here] = cross
        x0f = x0_ref[:, here].astype(F32)
        logit = logit + (x0f * cross + x0f) * head_ref[block : block + 1, :]
    logit = jnp.sum(logit, axis=1, keepdims=True)
    d_logit = column(weight_ref) * (jax.nn.sigmoid(logit) - column(label_ref))
    for block in range(blocks):
        here = slice(block * LANES, (block + 1) * LANES)
        x0f = x0_ref[:, here].astype(F32)
        x1 = x0f * cross_ref[:, here] + x0f
        grads_ref[0, block : block + 1, :] = jnp.sum(d_logit * x1, axis=0, keepdims=True)
        d_cross = d_logit * head_ref[block : block + 1, :] * x0f
        grads_ref[1, block : block + 1, :] = jnp.sum(d_cross, axis=0, keepdims=True)
        d_cross_ref[:, here] = d_cross.astype(BF16)
    d_low = lax.dot_general(
        d_cross_ref[...], up_ref[...], (((1,), (1,)), ((), ())), preferred_element_type=F32
    ).astype(BF16)
    for block in range(blocks):
        here = slice(block * LANES, (block + 1) * LANES)
        d_x1 = d_logit * head_ref[block : block + 1, :]
        d_x0 = d_x1 * (cross_ref[:, here] + 1.0) + lax.dot_general(
            d_low, down_ref[here, :], (((1,), (1,)), ((), ())), preferred_element_type=F32
        )
        if block == 0:
            dense_grad_ref[...] = d_x0.astype(BF16)
        else:
            place = slice((block - 1) * samples, block * samples)
            d_pooled_ref[place, :] = d_x0.astype(BF16)


def cross_layer(dense, own, other, far, labels, weights, down_w, up_w, bias, head):
    samples, width = dense.shape
    tables = own.shape[1] // samples
    cross = down_w.shape[0]
    return pl.pallas_call(
        functools.partial(cross_kernel, tables),
        out_shape=(
            jax.ShapeDtypeStruct((tables * samples, width), BF16),
            jax.ShapeDtypeStruct((samples, width), BF16),
            jax.ShapeDtypeStruct((2, cross // LANES, LANES), F32),
        ),
        scratch_shapes=[
            pltpu.VMEM((samples, cross), BF16),
            pltpu.VMEM((samples, cross), F32),
            pltpu.VMEM((samples, cross), BF16),
        ],
        compiler_params=params(),
        cost_estimate=cost(8 * 10**9, 12 * 10**6),
        name="cross_layer",
    )(dense, own, other, far, labels, weights, down_w, up_w, bias, head)


def spread_kernel(turns, count, at, *refs):
    sides = [refs[3 * i : 3 * i + 3] for i in range(count)]
    before = refs[3 * count : -1 - count]
    rows_ref, masked = refs[-1 - count], refs[-count:]
    zero = jnp.array(0, BF16)
    for (column_ref, gradient_ref, _), masked_ref in zip(sides, masked):
        for i, one in enumerate(turns):
            masked_ref[:, i * LANES : (i + 1) * LANES] = jnp.where(
                column_ref[...] == jnp.array(one, BF16), gradient_ref[...], zero
            )
    total = before[0][:, at * LANES : (at + len(turns)) * LANES] if before else None
    for (_, _, counts_ref), masked_ref in zip(sides, masked):
        part = jnp.dot(counts_ref[...], masked_ref[...], preferred_element_type=F32)
        total = part if total is None else total + part
    rows_ref[...] = total


def spread(turns, sides, before=None, at=0):
    bags, width = sides[0][1].shape
    rows = sides[0][2].shape[0]
    wide = len(turns) * width
    operands = [one for side in sides for one in side] + ([] if before is None else [before])
    return pl.pallas_call(
        functools.partial(spread_kernel, turns, len(sides), at),
        out_shape=jax.ShapeDtypeStruct((rows, wide), F32),
        in_specs=[VMEM] * len(operands),
        out_specs=VMEM,
        scratch_shapes=[pltpu.VMEM((bags, wide), BF16)] * len(sides),
        compiler_params=params(),
        cost_estimate=cost(0, 0),
        name="spread",
    )(*operands)


def place_kernel(at_ref, part_ref, *refs):
    rows_ref, sem = refs[-2], refs[-1]
    rows = part_ref.shape[0]
    start = pl.multiple_of(at_ref[0] * rows, rows)
    copy = pltpu.make_async_copy(part_ref, rows_ref.at[pl.ds(start, rows), :], sem)
    copy.start()
    copy.wait()


def place_half(at, part, before=None):
    rows, width = part.shape
    either = pl.BlockSpec(memory_space=pl.ANY)
    return pl.pallas_call(
        place_kernel,
        out_shape=jax.ShapeDtypeStruct((2 * rows, width), F32),
        in_specs=[pl.BlockSpec(memory_space=pltpu.SMEM), VMEM] + [either] * (before is not None),
        out_specs=either,
        scratch_shapes=[pltpu.SemaphoreType.DMA],
        input_output_aliases={} if before is None else {2: 0},
        compiler_params=params(),
        cost_estimate=cost(0, 0),
        name="place_half",
    )(at, part, *([] if before is None else [before]))


def swap(value, axis, stride):
    size = lax.axis_size(axis)
    return lax.ppermute(value, axis, [(i, i ^ stride) for i in range(size)])


def sum_pairs(value, axis, stride, wire):
    while stride < lax.axis_size(axis):
        value = value.astype(wire)
        value = value.astype(F32) + swap(value, axis, stride).astype(F32)
        stride *= 2
    return value


def ring_order(size):
    inner = 1 << ((size.bit_length() - 1) // 2)
    outer = size // inner
    cycle = []
    for far in range(outer):
        columns = range(1, inner) if far % 2 == 0 else range(inner - 1, 0, -1)
        cycle += [far * inner + column for column in columns]
    return cycle + [far * inner for far in range(outer - 1, -1, -1)]


def ring_turns(owners):
    order = ring_order(owners)
    right = [(order[i], order[(i + 1) % owners]) for i in range(owners)]
    return right, [(there, here) for here, there in right]


def count_and_pool(where, place, shard, local_rows, ahead):
    owners = lax.axis_size("emb")
    count = lambda own: bag_counts(where, own, owners, local_rows)
    places = [place, swap(place, "grp", 1)]
    sums = [None, None]

    def add(side, turns, shards, ahead=()):
        sums[side] = pool(turns, sides[side][1], sides[side][0], shards, sums[side], ahead)

    if owners != 8:
        sides = [count(one) for one in places]
        table = lax.all_gather(shard, "emb", axis=0, tiled=False)
        for start in range(0, owners, 8):
            here = tuple(range(start, start + 8))
            for side in (1, 0):
                add(side, here, [[table[one]] for one in here])
        sums[1] = swap(sums[1], "grp", 1)
        return sides, sums + [jnp.zeros_like(sums[1], BF16)]
    right, left = ring_turns(owners)
    lefts, rights = [shard], [shard]

    def step(beside):
        before = lefts[-1], rights[-1], beside
        a, b, beside = before if beside is None else lax.optimization_barrier(before)
        lefts.append(lax.ppermute(a, "emb", right))
        rights.append(lax.ppermute(b, "emb", left))
        return beside

    step(None)
    own, places[1] = step((count(places[0]), places[1]))
    near = (0, 1, 7), [[shard], [rights[1]], [lefts[1]]]
    *lent, sums[0] = bag_counts(
        where, places[1], owners, local_rows, near[0], (own[1], own[0]), [one for one, in near[1]]
    )
    *sides, sums[0] = step([own, lent, sums[0]])
    add(1, *near)
    add(1, (2, 6), [[rights[2]], [lefts[2]]], ahead)
    add(0, (2, 6), [[rights[2]], [lefts[2]]])
    middle = shard.shape[0] // 2
    a, b, sums[0], sums[1] = lax.optimization_barrier(
        (lefts[3][:middle], rights[3][middle:], sums[0], sums[1])
    )
    far = [lax.ppermute(a, "emb", right), lax.ppermute(b, "emb", left)]
    other, sums[1] = swap(sums[1], "grp", 1), None
    for side in (1, 0):
        add(side, (3, 5), [[rights[3]], [lefts[3]]])
    sums[0], sums[1] = lax.optimization_barrier((sums[0], sums[1]))
    lent = pool((4,), sides[1][1], sides[1][0], [far], sums[1], dtype=BF16)
    sums[1:] = other, swap(lent, "grp", 1)
    add(0, (4,), [far])
    return sides, sums


def spread_and_sum(sides, grads):
    owners = lax.axis_size("emb")
    width = sides[0][1].shape[1]
    exchanges = [
        (axis, 1 << bit)
        for axis in ("grp", "emb")
        for bit in range(lax.axis_size(axis).bit_length() - 1)
    ][1:]
    if owners != 8 or len(exchanges) != 4:
        parts = [
            spread(tuple(range(start, start + 4)), sides).astype(BF16)
            for start in range(0, owners, 4)
        ]
        for axis, stride in exchanges:
            grads = grads + swap(grads, axis, stride)
        part = lax.psum_scatter(
            jnp.concatenate(parts, axis=1), "emb", scatter_dimension=1, tiled=True
        )
        return sum_pairs(part, "grp", 2, BF16), grads
    right, left = ring_turns(owners)

    def exchange(grads):
        return grads + swap(grads, *exchanges.pop(0))

    def send(to_right, to_left):
        return lax.ppermute(to_right, "emb", right), lax.ppermute(to_left, "emb", left)

    def messages(part, went_right, went_left):
        to_right, to_left = part[:, :width], part[:, width:]
        return (to_right + went_right).astype(BF16), (to_left + went_left).astype(BF16)

    own = spread((4, 0), sides[:1])
    part = spread((4, 0), sides[1:], own)
    far, mine = part[:, :width].astype(BF16), part[:, width:]
    middle = far.shape[0] // 2
    far, sides, grads = lax.optimization_barrier((far, sides, grads))
    went_right, went_left = send(far[:middle], far[middle:])
    went_right = jnp.pad(went_right.astype(F32), ((0, middle), (0, 0)))
    went_left = jnp.pad(went_left.astype(F32), ((middle, 0), (0, 0)))
    for step in (3, 2, 1):
        part = spread((step, owners - step), sides)
        to_right, to_left = messages(part, went_right, went_left)
        to_right, to_left, sides, grads = lax.optimization_barrier((to_right, to_left, sides, grads))
        went_right, went_left = send(to_right, to_left)
        grads = exchange(grads)
        went_right, went_left = went_right.astype(F32), went_left.astype(F32)
    total = (mine + went_right + went_left).astype(BF16)
    total, grads = lax.optimization_barrier((total, grads))
    other, grads = lax.optimization_barrier((swap(total, "grp", 2), exchange(grads)))
    return total.astype(F32) + other.astype(F32), grads


def body(
    table_window,
    dense_part,
    bag_rows,
    bag_lengths,
    bag_owner,
    labels,
    sample_weight,
    down_w,
    up_w,
    cross_bias,
    head_w,
):
    samples, tables, hot = bag_rows.shape
    local_rows, width = table_window.shape
    rows = local_rows // 2
    half = (lax.axis_index("grp") % 2).astype(jnp.int32)
    where = jnp.stack([half, lax.axis_index("emb").astype(jnp.int32)])
    shard = lax.dynamic_slice_in_dim(table_window, half * rows, rows, 0)
    shard = shard.reshape(-1, LANES, width).transpose(0, 2, 1).reshape(rows, LANES)
    live = jnp.arange(hot, dtype=jnp.int32)[None, :, None] < bag_lengths.T[:, None, :]
    place = bag_owner.transpose(1, 2, 0) * local_rows + bag_rows.transpose(1, 2, 0)
    place = jnp.where(live, place, -1)
    sides, (own, other, far) = count_and_pool(where, place, shard, local_rows, (down_w, up_w))
    d_pooled, dense_grad, grads = cross_layer(
        dense_part,
        own,
        other,
        far,
        labels.astype(F32).reshape(1, samples),
        sample_weight.reshape(1, samples),
        down_w,
        up_w,
        cross_bias.reshape(-1, LANES),
        head_w.reshape(-1, LANES),
    )
    grads = grads + swap(grads, "grp", 1)
    sides = [
        (sides[0][2], d_pooled, sides[0][0]),
        (sides[1][2], swap(d_pooled, "grp", 1), sides[1][0]),
    ]
    row_half, grads = spread_and_sum(sides, grads)
    at = half.reshape(1)
    row_grad = place_half(1 - at, swap(row_half, "grp", 1), place_half(at, row_half))
    return (row_grad, grads[0].reshape(-1), grads[1].reshape(-1), dense_grad)


def solution(mesh):
    in_specs = (
        P("emb", None),
        P(("grp", "emb"), None),
        P(("grp", "emb"), None, None),
        P(("grp", "emb"), None),
        P(("grp", "emb"), None, None),
        P(("grp", "emb")),
        P(("grp", "emb")),
        P(),
        P(),
        P(),
        P(),
    )
    out_specs = (P("emb", None), P(), P(), P(("grp", "emb"), None))
    return jax.shard_map(body, mesh=mesh, in_specs=in_specs, out_specs=out_specs, check_vma=False)
```

```python
import functools

import jax
import jax.numpy as jnp
from jax import lax
from jax.experimental import pallas as pl
from jax.experimental.pallas import tpu as pltpu
from jax.sharding import PartitionSpec as P

BF16 = jnp.bfloat16
F32 = jnp.float32
LANES = 128
SPAN = 2
CHUNK = 32
VMEM_BYTES = 16 * 1024 * 1024


def params():
    return pltpu.CompilerParams(vmem_limit_bytes=VMEM_BYTES)


VMEM = pl.BlockSpec(memory_space=pltpu.VMEM)


def cost(flops, moved):
    return pl.CostEstimate(flops=flops, bytes_accessed=moved, transcendentals=0)


def ring_place(owner):
    return jnp.where(owner % 2 == 1, owner // 2, 7 - owner // 2)


def diagonal():
    return lax.broadcasted_iota(jnp.int32, (LANES, LANES), 0) == lax.broadcasted_iota(
        jnp.int32, (LANES, LANES), 1
    )


def side_by_side(blocks):
    tiles = [ref[row : row + LANES, :] for ref in blocks for row in range(0, ref.shape[0], LANES)]
    return jnp.concatenate(tiles, axis=1)


def count_kernel(owners, local_rows, turns, where_ref, place_ref, *refs):
    if turns:
        counts_ref, turn_ref, column_ref, sum_ref = refs[-4:]
        own_turn_ref, own_counts_ref, blocks = refs[0], refs[1], refs[2:-4]
    else:
        counts_ref, turn_ref, column_ref = refs
    tables, hot, _ = place_ref.shape
    rows = counts_ref.shape[0]
    high = rows // LANES
    half, index = where_ref[0], where_ref[1]
    shift = local_rows.bit_length() - 1
    eye = diagonal()
    ones = jnp.ones((LANES, LANES), BF16)
    ids = lax.broadcasted_iota(jnp.int32, (LANES, LANES), 0)

    def table(at, carry):
        place = place_ref[at]
        owner = place[0:1, :] >> shift
        if owners == 8:
            turn = (ring_place(owner) - ring_place(index) + owners) & (owners - 1)
        else:
            turn = owner
        turn = turn.astype(F32)
        turn_ref[pl.ds(at, 1), :] = turn
        lanes = pl.ds(pl.multiple_of(at * LANES, LANES), LANES)
        column_ref[lanes, :] = jnp.dot(
            jnp.where(eye, turn, 0.0).astype(BF16), ones, preferred_element_type=F32
        ).astype(BF16)
        here = (place & (local_rows - 1)) - half * rows
        inside = (place >= 0) & (here >= 0) & (here < rows)
        low = jnp.where(inside, here & (LANES - 1), -1)
        code = jnp.where(inside, jnp.left_shift(1, 4 * (here >> (LANES.bit_length() - 1))), 0)
        for first in range(0, LANES, CHUNK):
            total = 0
            for h in range(hot):
                total = total + jnp.where(
                    ids[first : first + CHUNK] == low[h : h + 1, :], code[h : h + 1, :], 0
                )
            for part in range(high):
                count = lax.shift_right_logical(total, 4 * part) & 15
                start = part * LANES + first
                counts_ref[start : start + CHUNK, lanes] = count.astype(F32).astype(BF16)
        return carry

    def pair(at, carry):
        lanes = pl.ds(pl.multiple_of(at * 2 * LANES, 2 * LANES), 2 * LANES)
        left = jnp.concatenate([side_by_side([block]) for block in blocks], axis=0)
        product = jnp.dot(left, own_counts_ref[:, lanes], preferred_element_type=F32)
        for one in range(2):
            table(2 * at + one, 0)
        total = []
        for one in range(2):
            turn = own_turn_ref[pl.ds(2 * at + one, 1), :]
            part = 0.0
            for i, each in enumerate(turns):
                mine = product[i * LANES : (i + 1) * LANES, one * LANES : (one + 1) * LANES]
                part = jnp.where(turn == each, mine, part)
            total.append(part)
        sum_ref[:, lanes] = jnp.concatenate(total, axis=1)
        return carry

    if turns:
        lax.fori_loop(0, tables // 2, pair, 0)
    else:
        lax.fori_loop(0, tables, table, 0, unroll=2)


def bag_counts(where, place, owners, local_rows, turns=(), own=(), shards=()):
    tables, hot, samples = place.shape
    bags = tables * samples
    rows = local_rows // 2
    operands = [*own, *shards] if turns else []
    out_shape = (
        jax.ShapeDtypeStruct((rows, bags), BF16),
        jax.ShapeDtypeStruct((tables, samples), F32),
        jax.ShapeDtypeStruct((bags, LANES), BF16),
    ) + ((jax.ShapeDtypeStruct((LANES, bags), F32),) if turns else ())
    return pl.pallas_call(
        functools.partial(count_kernel, owners, local_rows, turns),
        out_shape=out_shape,
        in_specs=[pl.BlockSpec(memory_space=pltpu.SMEM)] + [VMEM] * (1 + len(operands)),
        out_specs=(VMEM,) * len(out_shape),
        compiler_params=params(),
        cost_estimate=cost(5 * 10**9, 0),
        name="bag_counts",
    )(where, place, *operands)


def pool_kernel(shards, turns, tables, added, turn_ref, counts_ref, *refs):
    sum_ref = refs[-1]
    blocks = refs[: sum(shards)]
    before = refs[sum(shards) : sum(shards) + added]
    left, at = [], 0
    for parts in shards:
        left.append(side_by_side(blocks[at : at + parts]))
        at += parts
    left = jnp.concatenate(left, axis=0)
    for start in range(0, turn_ref.shape[0], tables):
        bags = slice(start * LANES, (start + tables) * LANES)
        product = jnp.dot(left, counts_ref[:, bags], preferred_element_type=F32)
        for table in range(tables):
            turn = turn_ref[start + table : start + table + 1, :]
            here = slice((start + table) * LANES, (start + table + 1) * LANES)
            total = before[0][:, here] if before else 0.0
            for i, one in enumerate(turns):
                mine = product[i * LANES : (i + 1) * LANES, table * LANES : (table + 1) * LANES]
                total = jnp.where(turn == one, mine, total)
            sum_ref[:, here] = total


def pool(turns, turn, counts, shards, before, ahead=()):
    rows, bags = counts.shape
    blocks = [block for shard in shards for block in shard]
    width = blocks[0].shape[1]
    tables = turn.shape[0]
    extra = ([] if before is None else [before]) + list(ahead)
    return pl.pallas_call(
        functools.partial(
            pool_kernel,
            [len(shard) for shard in shards],
            turns,
            tables if len(turns) <= 4 else tables // 2,
            0 if before is None else 1,
        ),
        out_shape=jax.ShapeDtypeStruct((width, bags), F32),
        in_specs=[VMEM] * (2 + len(blocks) + len(extra)),
        out_specs=VMEM,
        compiler_params=params(),
        cost_estimate=cost(0, 0),
        name="pool",
    )(turn, counts, *blocks, *extra)


def cross_kernel(
    tables,
    dense_ref,
    own_ref,
    other_ref,
    label_ref,
    weight_ref,
    down_ref,
    up_ref,
    bias_ref,
    head_ref,
    d_pooled_ref,
    dense_grad_ref,
    grads_ref,
    x0_ref,
    cross_ref,
    d_cross_ref,
):
    samples = dense_ref.shape[0]
    blocks = tables + 1
    eye = diagonal()
    column = lambda ref: jnp.sum(jnp.where(eye, ref[...], 0.0), axis=1, keepdims=True)
    x0_ref[:, :LANES] = dense_ref[...]
    for table in range(tables):
        here = slice(table * LANES, (table + 1) * LANES)
        x0_ref[:, (table + 1) * LANES : (table + 2) * LANES] = (
            (own_ref[:, here] + other_ref[:, here]).T.astype(BF16)
        )
    low = jnp.dot(x0_ref[...], down_ref[...], preferred_element_type=F32).astype(BF16)
    spans = [(block, min(block + SPAN, blocks)) for block in range(0, blocks, SPAN)]
    columns = lambda span: slice(span[0] * LANES, span[1] * LANES)
    row = lambda ref, span: jnp.concatenate([ref[i : i + 1, :] for i in range(*span)], axis=1)
    logit = jnp.zeros((samples, LANES), F32)
    for span in spans:
        here = columns(span)
        cross = jnp.dot(low, up_ref[:, here], preferred_element_type=F32) + row(bias_ref, span)
        cross_ref[:, here] = cross
        x0f = x0_ref[:, here].astype(F32)
        terms = (x0f * cross + x0f) * row(head_ref, span)
        for start in range(0, terms.shape[1], LANES):
            logit = logit + terms[:, start : start + LANES]
    logit = jnp.sum(logit, axis=1, keepdims=True)
    d_logit = column(weight_ref) * (jax.nn.sigmoid(logit) - column(label_ref))
    for block in range(blocks):
        here = slice(block * LANES, (block + 1) * LANES)
        x0f = x0_ref[:, here].astype(F32)
        x1 = x0f * cross_ref[:, here] + x0f
        grads_ref[0, block : block + 1, :] = jnp.sum(d_logit * x1, axis=0, keepdims=True)
        d_cross = d_logit * head_ref[block : block + 1, :] * x0f
        grads_ref[1, block : block + 1, :] = jnp.sum(d_cross, axis=0, keepdims=True)
        d_cross_ref[:, here] = d_cross.astype(BF16)
    d_low = lax.dot_general(
        d_cross_ref[...], up_ref[...], (((1,), (1,)), ((), ())), preferred_element_type=F32
    ).astype(BF16)
    for span in spans:
        here = columns(span)
        d_x1 = d_logit * row(head_ref, span)
        d_x0 = d_x1 * (cross_ref[:, here] + 1.0) + lax.dot_general(
            d_low, down_ref[here, :], (((1,), (1,)), ((), ())), preferred_element_type=F32
        )
        for block in range(*span):
            part = d_x0[:, (block - span[0]) * LANES : (block - span[0] + 1) * LANES]
            if block == 0:
                dense_grad_ref[...] = part.astype(BF16)
            else:
                d_pooled_ref[(block - 1) * samples : block * samples, :] = part.astype(BF16)


def cross_layer(dense, own, other, labels, weights, down_w, up_w, bias, head):
    samples, width = dense.shape
    tables = own.shape[1] // samples
    cross = down_w.shape[0]
    return pl.pallas_call(
        functools.partial(cross_kernel, tables),
        out_shape=(
            jax.ShapeDtypeStruct((tables * samples, width), BF16),
            jax.ShapeDtypeStruct((samples, width), BF16),
            jax.ShapeDtypeStruct((2, cross // LANES, LANES), F32),
        ),
        scratch_shapes=[
            pltpu.VMEM((samples, cross), BF16),
            pltpu.VMEM((samples, cross), F32),
            pltpu.VMEM((samples, cross), BF16),
        ],
        compiler_params=params(),
        cost_estimate=cost(8 * 10**9, 12 * 10**6),
        name="cross_layer",
    )(dense, own, other, labels, weights, down_w, up_w, bias, head)


def spread_kernel(turns, count, at, *refs):
    sides = [refs[3 * i : 3 * i + 3] for i in range(count)]
    before = refs[3 * count : -1 - count]
    rows_ref, masked = refs[-1 - count], refs[-count:]
    zero = jnp.array(0, BF16)
    for (column_ref, gradient_ref, _), masked_ref in zip(sides, masked):
        for i, one in enumerate(turns):
            masked_ref[:, i * LANES : (i + 1) * LANES] = jnp.where(
                column_ref[...] == jnp.array(one, BF16), gradient_ref[...], zero
            )
    total = before[0][:, at * LANES : (at + len(turns)) * LANES] if before else None
    for (_, _, counts_ref), masked_ref in zip(sides, masked):
        part = jnp.dot(counts_ref[...], masked_ref[...], preferred_element_type=F32)
        total = part if total is None else total + part
    rows_ref[...] = total


def spread(turns, sides, before=None, at=0):
    bags, width = sides[0][1].shape
    rows = sides[0][2].shape[0]
    wide = len(turns) * width
    operands = [one for side in sides for one in side] + ([] if before is None else [before])
    return pl.pallas_call(
        functools.partial(spread_kernel, turns, len(sides), at),
        out_shape=jax.ShapeDtypeStruct((rows, wide), F32),
        in_specs=[VMEM] * len(operands),
        out_specs=VMEM,
        scratch_shapes=[pltpu.VMEM((bags, wide), BF16)] * len(sides),
        compiler_params=params(),
        cost_estimate=cost(0, 0),
        name="spread",
    )(*operands)


def place_kernel(at_ref, part_ref, *refs):
    rows_ref, sem = refs[-2], refs[-1]
    rows = part_ref.shape[0]
    start = pl.multiple_of(at_ref[0] * rows, rows)
    copy = pltpu.make_async_copy(part_ref, rows_ref.at[pl.ds(start, rows), :], sem)
    copy.start()
    copy.wait()


def place_half(at, part, before=None):
    rows, width = part.shape
    either = pl.BlockSpec(memory_space=pl.ANY)
    return pl.pallas_call(
        place_kernel,
        out_shape=jax.ShapeDtypeStruct((2 * rows, width), F32),
        in_specs=[pl.BlockSpec(memory_space=pltpu.SMEM), VMEM] + [either] * (before is not None),
        out_specs=either,
        scratch_shapes=[pltpu.SemaphoreType.DMA],
        input_output_aliases={} if before is None else {2: 0},
        compiler_params=params(),
        cost_estimate=cost(0, 0),
        name="place_half",
    )(at, part, *([] if before is None else [before]))


def swap(value, axis, stride):
    size = lax.axis_size(axis)
    return lax.ppermute(value, axis, [(i, i ^ stride) for i in range(size)])


def sum_pairs(value, axis, stride, wire):
    while stride < lax.axis_size(axis):
        value = value.astype(wire)
        value = value.astype(F32) + swap(value, axis, stride).astype(F32)
        stride *= 2
    return value


def ring_order(size):
    inner = 1 << ((size.bit_length() - 1) // 2)
    outer = size // inner
    cycle = []
    for far in range(outer):
        columns = range(1, inner) if far % 2 == 0 else range(inner - 1, 0, -1)
        cycle += [far * inner + column for column in columns]
    return cycle + [far * inner for far in range(outer - 1, -1, -1)]


def ring_turns(owners):
    order = ring_order(owners)
    right = [(order[i], order[(i + 1) % owners]) for i in range(owners)]
    return right, [(there, here) for here, there in right]


def count_and_pool(where, place, shard, local_rows, ahead):
    owners = lax.axis_size("emb")
    count = lambda own: bag_counts(where, own, owners, local_rows)
    places = [place, swap(place, "grp", 1)]
    sums = [None, None]

    def add(side, turns, shards, ahead=()):
        sums[side] = pool(turns, sides[side][1], sides[side][0], shards, sums[side], ahead)

    if owners != 8:
        sides = [count(one) for one in places]
        table = lax.all_gather(shard, "emb", axis=0, tiled=False)
        for start in range(0, owners, 8):
            here = tuple(range(start, start + 8))
            for side in (1, 0):
                add(side, here, [[table[one]] for one in here])
        return sides, sums
    right, left = ring_turns(owners)
    lefts, rights = [shard], [shard]

    def step(beside):
        before = lefts[-1], rights[-1], beside
        a, b, beside = before if beside is None else lax.optimization_barrier(before)
        lefts.append(lax.ppermute(a, "emb", right))
        rights.append(lax.ppermute(b, "emb", left))
        return beside

    step(None)
    own, places[1] = step((count(places[0]), places[1]))
    near = (0, 1, 7), [[shard], [rights[1]], [lefts[1]]]
    *lent, sums[0] = bag_counts(
        where, places[1], owners, local_rows, near[0], (own[1], own[0]), [one for one, in near[1]]
    )
    *sides, sums[0] = step([own, lent, sums[0]])
    add(1, *near)
    add(1, (2, 6), [[rights[2]], [lefts[2]]], ahead)
    add(0, (2, 6), [[rights[2]], [lefts[2]]])
    middle = shard.shape[0] // 2
    a, b, sums[0], sums[1] = lax.optimization_barrier(
        (lefts[3][:middle], rights[3][middle:], sums[0], sums[1])
    )
    far = [lax.ppermute(a, "emb", right), lax.ppermute(b, "emb", left)]
    for side in (1, 0):
        add(side, (3, 5), [[rights[3]], [lefts[3]]])
    sums[0], sums[1] = lax.optimization_barrier((sums[0], sums[1]))
    for side in (1, 0):
        add(side, (4,), [far])
    return sides, sums


def spread_and_sum(sides, grads):
    owners = lax.axis_size("emb")
    width = sides[0][1].shape[1]
    exchanges = [
        (axis, 1 << bit)
        for axis in ("grp", "emb")
        for bit in range(lax.axis_size(axis).bit_length() - 1)
    ][1:]
    if owners != 8 or len(exchanges) != 4:
        parts = [
            spread(tuple(range(start, start + 4)), sides).astype(BF16)
            for start in range(0, owners, 4)
        ]
        for axis, stride in exchanges:
            grads = grads + swap(grads, axis, stride)
        part = lax.psum_scatter(
            jnp.concatenate(parts, axis=1), "emb", scatter_dimension=1, tiled=True
        )
        return sum_pairs(part, "grp", 2, BF16), grads
    right, left = ring_turns(owners)

    def exchange(grads):
        return grads + swap(grads, *exchanges.pop(0))

    def send(to_right, to_left):
        return lax.ppermute(to_right, "emb", right), lax.ppermute(to_left, "emb", left)

    def messages(part, went_right, went_left):
        to_right, to_left = part[:, :width], part[:, width:]
        return (to_right + went_right).astype(BF16), (to_left + went_left).astype(BF16)

    own = spread((4, 0), sides[:1])
    part = spread((4, 0), sides[1:], own)
    far, mine = part[:, :width].astype(BF16), part[:, width:]
    middle = far.shape[0] // 2
    far, sides, grads = lax.optimization_barrier((far, sides, grads))
    went_right, went_left = send(far[:middle], far[middle:])
    went_right = jnp.pad(went_right.astype(F32), ((0, middle), (0, 0)))
    went_left = jnp.pad(went_left.astype(F32), ((middle, 0), (0, 0)))
    for step in (3, 2, 1):
        part = spread((step, owners - step), sides)
        to_right, to_left = messages(part, went_right, went_left)
        to_right, to_left, sides, grads = lax.optimization_barrier((to_right, to_left, sides, grads))
        went_right, went_left = send(to_right, to_left)
        grads = exchange(grads)
        went_right, went_left = went_right.astype(F32), went_left.astype(F32)
    total = (mine + went_right + went_left).astype(BF16)
    total, grads = lax.optimization_barrier((total, grads))
    other, grads = lax.optimization_barrier((swap(total, "grp", 2), exchange(grads)))
    return total.astype(F32) + other.astype(F32), grads


def body(
    table_window,
    dense_part,
    bag_rows,
    bag_lengths,
    bag_owner,
    labels,
    sample_weight,
    down_w,
    up_w,
    cross_bias,
    head_w,
):
    samples, tables, hot = bag_rows.shape
    local_rows, width = table_window.shape
    rows = local_rows // 2
    half = (lax.axis_index("grp") % 2).astype(jnp.int32)
    where = jnp.stack([half, lax.axis_index("emb").astype(jnp.int32)])
    shard = lax.dynamic_slice_in_dim(table_window, half * rows, rows, 0)
    shard = shard.reshape(-1, LANES, width).transpose(0, 2, 1).reshape(rows, LANES)
    live = jnp.arange(hot, dtype=jnp.int32)[None, :, None] < bag_lengths.T[:, None, :]
    place = bag_owner.transpose(1, 2, 0) * local_rows + bag_rows.transpose(1, 2, 0)
    place = jnp.where(live, place, -1)
    sides, (own, lent) = count_and_pool(where, place, shard, local_rows, (down_w, up_w))
    other = swap(lent, "grp", 1)
    d_pooled, dense_grad, grads = cross_layer(
        dense_part,
        own,
        other,
        labels.astype(F32).reshape(1, samples),
        sample_weight.reshape(1, samples),
        down_w,
        up_w,
        cross_bias.reshape(-1, LANES),
        head_w.reshape(-1, LANES),
    )
    grads = grads + swap(grads, "grp", 1)
    sides = [
        (sides[0][2], d_pooled, sides[0][0]),
        (sides[1][2], swap(d_pooled, "grp", 1), sides[1][0]),
    ]
    row_half, grads = spread_and_sum(sides, grads)
    at = half.reshape(1)
    row_grad = place_half(1 - at, swap(row_half, "grp", 1), place_half(at, row_half))
    return (row_grad, grads[0].reshape(-1), grads[1].reshape(-1), dense_grad)


def solution(mesh):
    in_specs = (
        P("emb", None),
        P(("grp", "emb"), None),
        P(("grp", "emb"), None, None),
        P(("grp", "emb"), None),
        P(("grp", "emb"), None, None),
        P(("grp", "emb")),
        P(("grp", "emb")),
        P(),
        P(),
        P(),
        P(),
    )
    out_specs = (P("emb", None), P(), P(), P(("grp", "emb"), None))
    return jax.shard_map(body, mesh=mesh, in_specs=in_specs, out_specs=out_specs, check_vma=False)
```

```python
import functools

import jax
import jax.numpy as jnp
from jax import lax
from jax.experimental import pallas as pl
from jax.experimental.pallas import tpu as pltpu
from jax.sharding import PartitionSpec as P

BF16 = jnp.bfloat16
F32 = jnp.float32
LANES = 128
CHUNK = 32
VMEM_BYTES = 16 * 1024 * 1024


def params():
    return pltpu.CompilerParams(vmem_limit_bytes=VMEM_BYTES)


VMEM = pl.BlockSpec(memory_space=pltpu.VMEM)


def cost(flops, moved):
    return pl.CostEstimate(flops=flops, bytes_accessed=moved, transcendentals=0)


def ring_place(owner):
    return jnp.where(owner % 2 == 1, owner // 2, 7 - owner // 2)


def diagonal():
    return lax.broadcasted_iota(jnp.int32, (LANES, LANES), 0) == lax.broadcasted_iota(
        jnp.int32, (LANES, LANES), 1
    )


def side_by_side(blocks):
    tiles = [ref[row : row + LANES, :] for ref in blocks for row in range(0, ref.shape[0], LANES)]
    return jnp.concatenate(tiles, axis=1)


def count_kernel(owners, local_rows, turns, where_ref, place_ref, *refs):
    if turns:
        counts_ref, turn_ref, column_ref, sum_ref = refs[-4:]
        own_turn_ref, own_counts_ref, blocks = refs[0], refs[1], refs[2:-4]
    else:
        counts_ref, turn_ref, column_ref = refs
    tables, hot, _ = place_ref.shape
    rows = counts_ref.shape[0]
    high = rows // LANES
    half, index = where_ref[0], where_ref[1]
    shift = local_rows.bit_length() - 1
    eye = diagonal()
    ones = jnp.ones((LANES, LANES), BF16)
    ids = lax.broadcasted_iota(jnp.int32, (LANES, LANES), 0)

    def table(at, carry):
        place = place_ref[at]
        owner = place[0:1, :] >> shift
        if owners == 8:
            turn = (ring_place(owner) - ring_place(index) + owners) & (owners - 1)
        else:
            turn = owner
        turn = turn.astype(F32)
        turn_ref[pl.ds(at, 1), :] = turn
        lanes = pl.ds(pl.multiple_of(at * LANES, LANES), LANES)
        column_ref[lanes, :] = jnp.dot(
            jnp.where(eye, turn, 0.0).astype(BF16), ones, preferred_element_type=F32
        ).astype(BF16)
        here = (place & (local_rows - 1)) - half * rows
        inside = (place >= 0) & (here >= 0) & (here < rows)
        low = jnp.where(inside, here & (LANES - 1), -1)
        code = jnp.where(inside, jnp.left_shift(1, 4 * (here >> (LANES.bit_length() - 1))), 0)
        for first in range(0, LANES, CHUNK):
            total = 0
            for h in range(hot):
                total = total + jnp.where(
                    ids[first : first + CHUNK] == low[h : h + 1, :], code[h : h + 1, :], 0
                )
            for part in range(high):
                count = lax.shift_right_logical(total, 4 * part) & 15
                start = part * LANES + first
                counts_ref[start : start + CHUNK, lanes] = count.astype(F32).astype(BF16)
        return carry

    def pair(at, carry):
        lanes = pl.ds(pl.multiple_of(at * 2 * LANES, 2 * LANES), 2 * LANES)
        left = jnp.concatenate([side_by_side([block]) for block in blocks], axis=0)
        product = jnp.dot(left, own_counts_ref[:, lanes], preferred_element_type=F32)
        for one in range(2):
            table(2 * at + one, 0)
        total = []
        for one in range(2):
            turn = own_turn_ref[pl.ds(2 * at + one, 1), :]
            part = 0.0
            for i, each in enumerate(turns):
                mine = product[i * LANES : (i + 1) * LANES, one * LANES : (one + 1) * LANES]
                part = jnp.where(turn == each, mine, part)
            total.append(part)
        sum_ref[:, lanes] = jnp.concatenate(total, axis=1)
        return carry

    if turns:
        lax.fori_loop(0, tables // 2, pair, 0)
    else:
        lax.fori_loop(0, tables, table, 0, unroll=2)


def bag_counts(where, place, owners, local_rows, turns=(), own=(), shards=()):
    tables, hot, samples = place.shape
    bags = tables * samples
    rows = local_rows // 2
    operands = [*own, *shards] if turns else []
    out_shape = (
        jax.ShapeDtypeStruct((rows, bags), BF16),
        jax.ShapeDtypeStruct((tables, samples), F32),
        jax.ShapeDtypeStruct((bags, LANES), BF16),
    ) + ((jax.ShapeDtypeStruct((LANES, bags), F32),) if turns else ())
    return pl.pallas_call(
        functools.partial(count_kernel, owners, local_rows, turns),
        out_shape=out_shape,
        in_specs=[pl.BlockSpec(memory_space=pltpu.SMEM)] + [VMEM] * (1 + len(operands)),
        out_specs=(VMEM,) * len(out_shape),
        compiler_params=params(),
        cost_estimate=cost(5 * 10**9, 0),
        name="bag_counts",
    )(where, place, *operands)


def pool_kernel(shards, turns, tables, added, span, turn_ref, counts_ref, *refs):
    sum_ref = refs[-1]
    blocks = refs[: sum(shards)]
    before = refs[sum(shards) : sum(shards) + added]
    left, at = [], 0
    for parts in shards:
        left.append(side_by_side(blocks[at : at + parts]))
        at += parts
    left = jnp.concatenate(left, axis=0)
    for start in range(*span, tables):
        bags = slice(start * LANES, (start + tables) * LANES)
        product = jnp.dot(left, counts_ref[:, bags], preferred_element_type=F32)
        for table in range(tables):
            turn = turn_ref[start + table : start + table + 1, :]
            here = slice((start + table) * LANES, (start + table + 1) * LANES)
            total = before[0][:, here] if before else 0.0
            for i, one in enumerate(turns):
                mine = product[i * LANES : (i + 1) * LANES, table * LANES : (table + 1) * LANES]
                total = jnp.where(turn == one, mine, total)
            place = start + table - span[0]
            sum_ref[:, place * LANES : (place + 1) * LANES] = total


def pool(turns, turn, counts, shards, before, ahead=(), span=None):
    rows, bags = counts.shape
    blocks = [block for shard in shards for block in shard]
    width = blocks[0].shape[1]
    first, last = span or (0, turn.shape[0])
    extra = ([] if before is None else [before]) + list(ahead)
    return pl.pallas_call(
        functools.partial(
            pool_kernel,
            [len(shard) for shard in shards],
            turns,
            (last - first) if len(turns) <= 4 else (last - first) // 2,
            0 if before is None else 1,
            (first, last),
        ),
        out_shape=jax.ShapeDtypeStruct((width, (last - first) * LANES), F32),
        in_specs=[VMEM] * (2 + len(blocks) + len(extra)),
        out_specs=VMEM,
        compiler_params=params(),
        cost_estimate=cost(0, 0),
        name="pool",
    )(turn, counts, *blocks, *extra)


def cross_kernel(
    tables,
    dense_ref,
    own_ref,
    first_ref,
    second_ref,
    label_ref,
    weight_ref,
    down_ref,
    up_ref,
    bias_ref,
    head_ref,
    d_pooled_ref,
    dense_grad_ref,
    grads_ref,
    x0_ref,
    cross_ref,
    d_cross_ref,
):
    samples = dense_ref.shape[0]
    blocks = tables + 1
    eye = diagonal()
    column = lambda ref: jnp.sum(jnp.where(eye, ref[...], 0.0), axis=1, keepdims=True)
    x0_ref[:, :LANES] = dense_ref[...]
    for table in range(tables):
        here = slice(table * LANES, (table + 1) * LANES)
        part, start = (first_ref, 0) if table < tables // 2 else (second_ref, tables // 2)
        other = part[:, (table - start) * LANES : (table - start + 1) * LANES]
        x0_ref[:, (table + 1) * LANES : (table + 2) * LANES] = (
            (own_ref[:, here] + other).T.astype(BF16)
        )
    low = jnp.dot(x0_ref[...], down_ref[...], preferred_element_type=F32).astype(BF16)
    logit = jnp.zeros((samples, LANES), F32)
    for block in range(blocks):
        here = slice(block * LANES, (block + 1) * LANES)
        cross = jnp.dot(low, up_ref[:, here], preferred_element_type=F32) + bias_ref[block : block + 1, :]
        cross_ref[:, here] = cross
        x0f = x0_ref[:, here].astype(F32)
        logit = logit + (x0f * cross + x0f) * head_ref[block : block + 1, :]
    logit = jnp.sum(logit, axis=1, keepdims=True)
    d_logit = column(weight_ref) * (jax.nn.sigmoid(logit) - column(label_ref))
    for block in range(blocks):
        here = slice(block * LANES, (block + 1) * LANES)
        x0f = x0_ref[:, here].astype(F32)
        x1 = x0f * cross_ref[:, here] + x0f
        grads_ref[0, block : block + 1, :] = jnp.sum(d_logit * x1, axis=0, keepdims=True)
        d_cross = d_logit * head_ref[block : block + 1, :] * x0f
        grads_ref[1, block : block + 1, :] = jnp.sum(d_cross, axis=0, keepdims=True)
        d_cross_ref[:, here] = d_cross.astype(BF16)
    d_low = lax.dot_general(
        d_cross_ref[...], up_ref[...], (((1,), (1,)), ((), ())), preferred_element_type=F32
    ).astype(BF16)
    for block in range(blocks):
        here = slice(block * LANES, (block + 1) * LANES)
        d_x1 = d_logit * head_ref[block : block + 1, :]
        d_x0 = d_x1 * (cross_ref[:, here] + 1.0) + lax.dot_general(
            d_low, down_ref[here, :], (((1,), (1,)), ((), ())), preferred_element_type=F32
        )
        if block == 0:
            dense_grad_ref[...] = d_x0.astype(BF16)
        else:
            place = slice((block - 1) * samples, block * samples)
            d_pooled_ref[place, :] = d_x0.astype(BF16)


def cross_layer(dense, own, first, second, labels, weights, down_w, up_w, bias, head):
    samples, width = dense.shape
    tables = own.shape[1] // samples
    cross = down_w.shape[0]
    return pl.pallas_call(
        functools.partial(cross_kernel, tables),
        out_shape=(
            jax.ShapeDtypeStruct((tables * samples, width), BF16),
            jax.ShapeDtypeStruct((samples, width), BF16),
            jax.ShapeDtypeStruct((2, cross // LANES, LANES), F32),
        ),
        scratch_shapes=[
            pltpu.VMEM((samples, cross), BF16),
            pltpu.VMEM((samples, cross), F32),
            pltpu.VMEM((samples, cross), BF16),
        ],
        compiler_params=params(),
        cost_estimate=cost(8 * 10**9, 12 * 10**6),
        name="cross_layer",
    )(dense, own, first, second, labels, weights, down_w, up_w, bias, head)


def spread_kernel(turns, count, at, *refs):
    sides = [refs[3 * i : 3 * i + 3] for i in range(count)]
    before = refs[3 * count : -1 - count]
    rows_ref, masked = refs[-1 - count], refs[-count:]
    zero = jnp.array(0, BF16)
    for (column_ref, gradient_ref, _), masked_ref in zip(sides, masked):
        for i, one in enumerate(turns):
            masked_ref[:, i * LANES : (i + 1) * LANES] = jnp.where(
                column_ref[...] == jnp.array(one, BF16), gradient_ref[...], zero
            )
    total = before[0][:, at * LANES : (at + len(turns)) * LANES] if before else None
    for (_, _, counts_ref), masked_ref in zip(sides, masked):
        part = jnp.dot(counts_ref[...], masked_ref[...], preferred_element_type=F32)
        total = part if total is None else total + part
    rows_ref[...] = total


def spread(turns, sides, before=None, at=0):
    bags, width = sides[0][1].shape
    rows = sides[0][2].shape[0]
    wide = len(turns) * width
    operands = [one for side in sides for one in side] + ([] if before is None else [before])
    return pl.pallas_call(
        functools.partial(spread_kernel, turns, len(sides), at),
        out_shape=jax.ShapeDtypeStruct((rows, wide), F32),
        in_specs=[VMEM] * len(operands),
        out_specs=VMEM,
        scratch_shapes=[pltpu.VMEM((bags, wide), BF16)] * len(sides),
        compiler_params=params(),
        cost_estimate=cost(0, 0),
        name="spread",
    )(*operands)


def place_kernel(at_ref, part_ref, *refs):
    rows_ref, sem = refs[-2], refs[-1]
    rows = part_ref.shape[0]
    start = pl.multiple_of(at_ref[0] * rows, rows)
    copy = pltpu.make_async_copy(part_ref, rows_ref.at[pl.ds(start, rows), :], sem)
    copy.start()
    copy.wait()


def place_half(at, part, before=None):
    rows, width = part.shape
    either = pl.BlockSpec(memory_space=pl.ANY)
    return pl.pallas_call(
        place_kernel,
        out_shape=jax.ShapeDtypeStruct((2 * rows, width), F32),
        in_specs=[pl.BlockSpec(memory_space=pltpu.SMEM), VMEM] + [either] * (before is not None),
        out_specs=either,
        scratch_shapes=[pltpu.SemaphoreType.DMA],
        input_output_aliases={} if before is None else {2: 0},
        compiler_params=params(),
        cost_estimate=cost(0, 0),
        name="place_half",
    )(at, part, *([] if before is None else [before]))


def swap(value, axis, stride):
    size = lax.axis_size(axis)
    return lax.ppermute(value, axis, [(i, i ^ stride) for i in range(size)])


def sum_pairs(value, axis, stride, wire):
    while stride < lax.axis_size(axis):
        value = value.astype(wire)
        value = value.astype(F32) + swap(value, axis, stride).astype(F32)
        stride *= 2
    return value


def ring_order(size):
    inner = 1 << ((size.bit_length() - 1) // 2)
    outer = size // inner
    cycle = []
    for far in range(outer):
        columns = range(1, inner) if far % 2 == 0 else range(inner - 1, 0, -1)
        cycle += [far * inner + column for column in columns]
    return cycle + [far * inner for far in range(outer - 1, -1, -1)]


def ring_turns(owners):
    order = ring_order(owners)
    right = [(order[i], order[(i + 1) % owners]) for i in range(owners)]
    return right, [(there, here) for here, there in right]


def count_and_pool(where, place, shard, local_rows, ahead):
    owners = lax.axis_size("emb")
    count = lambda own: bag_counts(where, own, owners, local_rows)
    places = [place, swap(place, "grp", 1)]
    sums = [None, None]

    def add(side, turns, shards, ahead=()):
        sums[side] = pool(turns, sides[side][1], sides[side][0], shards, sums[side], ahead)

    if owners != 8:
        sides = [count(one) for one in places]
        table = lax.all_gather(shard, "emb", axis=0, tiled=False)
        for start in range(0, owners, 8):
            here = tuple(range(start, start + 8))
            for side in (1, 0):
                add(side, here, [[table[one]] for one in here])
        sums[1] = [swap(one, "grp", 1) for one in jnp.split(sums[1], 2, axis=1)]
        return sides, sums
    right, left = ring_turns(owners)
    lefts, rights = [shard], [shard]

    def step(beside):
        before = lefts[-1], rights[-1], beside
        a, b, beside = before if beside is None else lax.optimization_barrier(before)
        lefts.append(lax.ppermute(a, "emb", right))
        rights.append(lax.ppermute(b, "emb", left))
        return beside

    step(None)
    own, places[1] = step((count(places[0]), places[1]))
    near = (0, 1, 7), [[shard], [rights[1]], [lefts[1]]]
    *lent, sums[0] = bag_counts(
        where, places[1], owners, local_rows, near[0], (own[1], own[0]), [one for one, in near[1]]
    )
    *sides, sums[0] = step([own, lent, sums[0]])
    add(1, *near)
    add(1, (2, 6), [[rights[2]], [lefts[2]]], ahead)
    add(0, (2, 6), [[rights[2]], [lefts[2]]])
    middle = shard.shape[0] // 2
    a, b, sums[0], sums[1] = lax.optimization_barrier(
        (lefts[3][:middle], rights[3][middle:], sums[0], sums[1])
    )
    far = [lax.ppermute(a, "emb", right), lax.ppermute(b, "emb", left)]
    for side in (1, 0):
        add(side, (3, 5), [[rights[3]], [lefts[3]]])
    sums[0], sums[1] = lax.optimization_barrier((sums[0], sums[1]))
    turn, lent, tables = sides[1][1], sums[1], places[0].shape[0]
    sums[1] = [
        swap(pool((4,), turn, sides[1][0], [far], lent, span=span), "grp", 1)
        for span in ((0, tables // 2), (tables // 2, tables))
    ]
    add(0, (4,), [far])
    return sides, sums


def spread_and_sum(sides, grads):
    owners = lax.axis_size("emb")
    width = sides[0][1].shape[1]
    exchanges = [
        (axis, 1 << bit)
        for axis in ("grp", "emb")
        for bit in range(lax.axis_size(axis).bit_length() - 1)
    ][1:]
    if owners != 8 or len(exchanges) != 4:
        parts = [
            spread(tuple(range(start, start + 4)), sides).astype(BF16)
            for start in range(0, owners, 4)
        ]
        for axis, stride in exchanges:
            grads = grads + swap(grads, axis, stride)
        part = lax.psum_scatter(
            jnp.concatenate(parts, axis=1), "emb", scatter_dimension=1, tiled=True
        )
        return sum_pairs(part, "grp", 2, BF16), grads
    right, left = ring_turns(owners)

    def exchange(grads):
        return grads + swap(grads, *exchanges.pop(0))

    def send(to_right, to_left):
        return lax.ppermute(to_right, "emb", right), lax.ppermute(to_left, "emb", left)

    def messages(part, went_right, went_left):
        to_right, to_left = part[:, :width], part[:, width:]
        return (to_right + went_right).astype(BF16), (to_left + went_left).astype(BF16)

    own = spread((4, 0), sides[:1])
    part = spread((4, 0), sides[1:], own)
    far, mine = part[:, :width].astype(BF16), part[:, width:]
    middle = far.shape[0] // 2
    far, sides, grads = lax.optimization_barrier((far, sides, grads))
    went_right, went_left = send(far[:middle], far[middle:])
    went_right = jnp.pad(went_right.astype(F32), ((0, middle), (0, 0)))
    went_left = jnp.pad(went_left.astype(F32), ((middle, 0), (0, 0)))
    for step in (3, 2, 1):
        part = spread((step, owners - step), sides)
        to_right, to_left = messages(part, went_right, went_left)
        to_right, to_left, sides, grads = lax.optimization_barrier((to_right, to_left, sides, grads))
        went_right, went_left = send(to_right, to_left)
        grads = exchange(grads)
        went_right, went_left = went_right.astype(F32), went_left.astype(F32)
    total = (mine + went_right + went_left).astype(BF16)
    total, grads = lax.optimization_barrier((total, grads))
    other, grads = lax.optimization_barrier((swap(total, "grp", 2), exchange(grads)))
    return total.astype(F32) + other.astype(F32), grads


def body(
    table_window,
    dense_part,
    bag_rows,
    bag_lengths,
    bag_owner,
    labels,
    sample_weight,
    down_w,
    up_w,
    cross_bias,
    head_w,
):
    samples, tables, hot = bag_rows.shape
    local_rows, width = table_window.shape
    rows = local_rows // 2
    half = (lax.axis_index("grp") % 2).astype(jnp.int32)
    where = jnp.stack([half, lax.axis_index("emb").astype(jnp.int32)])
    shard = lax.dynamic_slice_in_dim(table_window, half * rows, rows, 0)
    shard = shard.reshape(-1, LANES, width).transpose(0, 2, 1).reshape(rows, LANES)
    live = jnp.arange(hot, dtype=jnp.int32)[None, :, None] < bag_lengths.T[:, None, :]
    place = bag_owner.transpose(1, 2, 0) * local_rows + bag_rows.transpose(1, 2, 0)
    place = jnp.where(live, place, -1)
    sides, (own, other) = count_and_pool(where, place, shard, local_rows, (down_w, up_w))
    d_pooled, dense_grad, grads = cross_layer(
        dense_part,
        own,
        *other,
        labels.astype(F32).reshape(1, samples),
        sample_weight.reshape(1, samples),
        down_w,
        up_w,
        cross_bias.reshape(-1, LANES),
        head_w.reshape(-1, LANES),
    )
    grads = grads + swap(grads, "grp", 1)
    sides = [
        (sides[0][2], d_pooled, sides[0][0]),
        (sides[1][2], swap(d_pooled, "grp", 1), sides[1][0]),
    ]
    row_half, grads = spread_and_sum(sides, grads)
    at = half.reshape(1)
    row_grad = place_half(1 - at, swap(row_half, "grp", 1), place_half(at, row_half))
    return (row_grad, grads[0].reshape(-1), grads[1].reshape(-1), dense_grad)


def solution(mesh):
    in_specs = (
        P("emb", None),
        P(("grp", "emb"), None),
        P(("grp", "emb"), None, None),
        P(("grp", "emb"), None),
        P(("grp", "emb"), None, None),
        P(("grp", "emb")),
        P(("grp", "emb")),
        P(),
        P(),
        P(),
        P(),
    )
    out_specs = (P("emb", None), P(), P(), P(("grp", "emb"), None))
    return jax.shard_map(body, mesh=mesh, in_specs=in_specs, out_specs=out_specs, check_vma=False)
```

```python
import functools

import jax
import jax.numpy as jnp
from jax import lax
from jax.experimental import pallas as pl
from jax.experimental.pallas import tpu as pltpu
from jax.sharding import PartitionSpec as P

BF16 = jnp.bfloat16
F32 = jnp.float32
LANES = 128
RING = ("grp", "emb")
CHUNK = 32
VMEM_BYTES = 16 * 1024 * 1024


def params():
    return pltpu.CompilerParams(vmem_limit_bytes=VMEM_BYTES)


VMEM = pl.BlockSpec(memory_space=pltpu.VMEM)


def cost(flops, moved):
    return pl.CostEstimate(flops=flops, bytes_accessed=moved, transcendentals=0)


def ring_place(owner):
    return jnp.where(owner % 2 == 1, owner // 2, 7 - owner // 2)


def diagonal():
    return lax.broadcasted_iota(jnp.int32, (LANES, LANES), 0) == lax.broadcasted_iota(
        jnp.int32, (LANES, LANES), 1
    )


def side_by_side(blocks):
    tiles = [ref[row : row + LANES, :] for ref in blocks for row in range(0, ref.shape[0], LANES)]
    return jnp.concatenate(tiles, axis=1)


def count_kernel(owners, local_rows, turns, where_ref, place_ref, *refs):
    if turns:
        counts_ref, turn_ref, column_ref, sum_ref = refs[-4:]
        own_turn_ref, own_counts_ref, blocks = refs[0], refs[1], refs[2:-4]
    else:
        counts_ref, turn_ref, column_ref = refs
    tables, hot, _ = place_ref.shape
    rows = counts_ref.shape[0]
    high = rows // LANES
    half, index = where_ref[0], where_ref[1]
    shift = local_rows.bit_length() - 1
    eye = diagonal()
    ones = jnp.ones((LANES, LANES), BF16)
    ids = lax.broadcasted_iota(jnp.int32, (LANES, LANES), 0)

    def table(at, carry):
        place = place_ref[at]
        owner = place[0:1, :] >> shift
        if owners == 8:
            turn = ring_place(owner) - ring_place(index)
            turn = jnp.where(half == 0, turn, -turn) & (owners - 1)
        else:
            turn = owner
        turn = turn.astype(F32)
        turn_ref[pl.ds(at, 1), :] = turn
        lanes = pl.ds(pl.multiple_of(at * LANES, LANES), LANES)
        column_ref[lanes, :] = jnp.dot(
            jnp.where(eye, turn, 0.0).astype(BF16), ones, preferred_element_type=F32
        ).astype(BF16)
        here = (place & (local_rows - 1)) - half * rows
        inside = (place >= 0) & (here >= 0) & (here < rows)
        low = jnp.where(inside, here & (LANES - 1), -1)
        code = jnp.where(inside, jnp.left_shift(1, 4 * (here >> (LANES.bit_length() - 1))), 0)
        for first in range(0, LANES, CHUNK):
            total = 0
            for h in range(hot):
                total = total + jnp.where(
                    ids[first : first + CHUNK] == low[h : h + 1, :], code[h : h + 1, :], 0
                )
            for part in range(high):
                count = lax.shift_right_logical(total, 4 * part) & 15
                start = part * LANES + first
                counts_ref[start : start + CHUNK, lanes] = count.astype(F32).astype(BF16)
        return carry

    def pair(at, carry):
        lanes = pl.ds(pl.multiple_of(at * 2 * LANES, 2 * LANES), 2 * LANES)
        left = jnp.concatenate([side_by_side([block]) for block in blocks], axis=0)
        product = jnp.dot(left, own_counts_ref[:, lanes], preferred_element_type=F32)
        for one in range(2):
            table(2 * at + one, 0)
        total = []
        for one in range(2):
            turn = own_turn_ref[pl.ds(2 * at + one, 1), :]
            part = 0.0
            for i, each in enumerate(turns):
                mine = product[i * LANES : (i + 1) * LANES, one * LANES : (one + 1) * LANES]
                part = jnp.where(turn == each, mine, part)
            total.append(part)
        sum_ref[:, lanes] = jnp.concatenate(total, axis=1)
        return carry

    if turns:
        lax.fori_loop(0, tables // 2, pair, 0)
    else:
        lax.fori_loop(0, tables, table, 0, unroll=2)


def bag_counts(where, place, owners, local_rows, turns=(), own=(), shards=()):
    tables, hot, samples = place.shape
    bags = tables * samples
    rows = local_rows // 2
    operands = [*own, *shards] if turns else []
    out_shape = (
        jax.ShapeDtypeStruct((rows, bags), BF16),
        jax.ShapeDtypeStruct((tables, samples), F32),
        jax.ShapeDtypeStruct((bags, LANES), BF16),
    ) + ((jax.ShapeDtypeStruct((LANES, bags), F32),) if turns else ())
    return pl.pallas_call(
        functools.partial(count_kernel, owners, local_rows, turns),
        out_shape=out_shape,
        in_specs=[pl.BlockSpec(memory_space=pltpu.SMEM)] + [VMEM] * (1 + len(operands)),
        out_specs=(VMEM,) * len(out_shape),
        compiler_params=params(),
        cost_estimate=cost(5 * 10**9, 0),
        name="bag_counts",
    )(where, place, *operands)


def pool_kernel(shards, turns, tables, added, span, turn_ref, counts_ref, *refs):
    sum_ref = refs[-1]
    blocks = refs[: sum(shards)]
    before = refs[sum(shards) : sum(shards) + added]
    left, at = [], 0
    for parts in shards:
        left.append(side_by_side(blocks[at : at + parts]))
        at += parts
    left = jnp.concatenate(left, axis=0)
    for start in range(*span, tables):
        bags = slice(start * LANES, (start + tables) * LANES)
        product = jnp.dot(left, counts_ref[:, bags], preferred_element_type=F32)
        for table in range(tables):
            turn = turn_ref[start + table : start + table + 1, :]
            here = slice((start + table) * LANES, (start + table + 1) * LANES)
            total = before[0][:, here] if before else 0.0
            for i, one in enumerate(turns):
                mine = product[i * LANES : (i + 1) * LANES, table * LANES : (table + 1) * LANES]
                total = jnp.where(turn == one, mine, total)
            place = start + table - span[0]
            sum_ref[:, place * LANES : (place + 1) * LANES] = total


def pool(turns, turn, counts, shards, before, ahead=(), span=None):
    rows, bags = counts.shape
    blocks = [block for shard in shards for block in shard]
    width = blocks[0].shape[1]
    first, last = span or (0, turn.shape[0])
    extra = ([] if before is None else [before]) + list(ahead)
    return pl.pallas_call(
        functools.partial(
            pool_kernel,
            [len(shard) for shard in shards],
            turns,
            (last - first) if len(turns) <= 4 else (last - first) // 2,
            0 if before is None else 1,
            (first, last),
        ),
        out_shape=jax.ShapeDtypeStruct((width, (last - first) * LANES), F32),
        in_specs=[VMEM] * (2 + len(blocks) + len(extra)),
        out_specs=VMEM,
        compiler_params=params(),
        cost_estimate=cost(0, 0),
        name="pool",
    )(turn, counts, *blocks, *extra)


def cross_kernel(
    tables,
    dense_ref,
    own_ref,
    first_ref,
    second_ref,
    label_ref,
    weight_ref,
    down_ref,
    up_ref,
    bias_ref,
    head_ref,
    d_pooled_ref,
    dense_grad_ref,
    grads_ref,
    x0_ref,
    cross_ref,
    d_cross_ref,
):
    samples = dense_ref.shape[0]
    blocks = tables + 1
    eye = diagonal()
    column = lambda ref: jnp.sum(jnp.where(eye, ref[...], 0.0), axis=1, keepdims=True)
    x0_ref[:, :LANES] = dense_ref[...]
    for table in range(tables):
        here = slice(table * LANES, (table + 1) * LANES)
        part, start = (first_ref, 0) if table < tables // 2 else (second_ref, tables // 2)
        other = part[:, (table - start) * LANES : (table - start + 1) * LANES]
        x0_ref[:, (table + 1) * LANES : (table + 2) * LANES] = (
            (own_ref[:, here] + other).T.astype(BF16)
        )
    low = jnp.dot(x0_ref[...], down_ref[...], preferred_element_type=F32).astype(BF16)
    logit = jnp.zeros((samples, LANES), F32)
    for block in range(blocks):
        here = slice(block * LANES, (block + 1) * LANES)
        cross = jnp.dot(low, up_ref[:, here], preferred_element_type=F32) + bias_ref[block : block + 1, :]
        cross_ref[:, here] = cross
        x0f = x0_ref[:, here].astype(F32)
        logit = logit + (x0f * cross + x0f) * head_ref[block : block + 1, :]
    logit = jnp.sum(logit, axis=1, keepdims=True)
    d_logit = column(weight_ref) * (jax.nn.sigmoid(logit) - column(label_ref))
    for block in range(blocks):
        here = slice(block * LANES, (block + 1) * LANES)
        x0f = x0_ref[:, here].astype(F32)
        x1 = x0f * cross_ref[:, here] + x0f
        grads_ref[0, block : block + 1, :] = jnp.sum(d_logit * x1, axis=0, keepdims=True)
        d_cross = d_logit * head_ref[block : block + 1, :] * x0f
        grads_ref[1, block : block + 1, :] = jnp.sum(d_cross, axis=0, keepdims=True)
        d_cross_ref[:, here] = d_cross.astype(BF16)
    d_low = lax.dot_general(
        d_cross_ref[...], up_ref[...], (((1,), (1,)), ((), ())), preferred_element_type=F32
    ).astype(BF16)
    for block in range(blocks):
        here = slice(block * LANES, (block + 1) * LANES)
        d_x1 = d_logit * head_ref[block : block + 1, :]
        d_x0 = d_x1 * (cross_ref[:, here] + 1.0) + lax.dot_general(
            d_low, down_ref[here, :], (((1,), (1,)), ((), ())), preferred_element_type=F32
        )
        if block == 0:
            dense_grad_ref[...] = d_x0.astype(BF16)
        else:
            place = slice((block - 1) * samples, block * samples)
            d_pooled_ref[place, :] = d_x0.astype(BF16)


def cross_layer(dense, own, first, second, labels, weights, down_w, up_w, bias, head):
    samples, width = dense.shape
    tables = own.shape[1] // samples
    cross = down_w.shape[0]
    return pl.pallas_call(
        functools.partial(cross_kernel, tables),
        out_shape=(
            jax.ShapeDtypeStruct((tables * samples, width), BF16),
            jax.ShapeDtypeStruct((samples, width), BF16),
            jax.ShapeDtypeStruct((2, cross // LANES, LANES), F32),
        ),
        scratch_shapes=[
            pltpu.VMEM((samples, cross), BF16),
            pltpu.VMEM((samples, cross), F32),
            pltpu.VMEM((samples, cross), BF16),
        ],
        compiler_params=params(),
        cost_estimate=cost(8 * 10**9, 12 * 10**6),
        name="cross_layer",
    )(dense, own, first, second, labels, weights, down_w, up_w, bias, head)


def spread_kernel(turns, count, at, *refs):
    sides = [refs[3 * i : 3 * i + 3] for i in range(count)]
    before = refs[3 * count : -1 - count]
    rows_ref, masked = refs[-1 - count], refs[-count:]
    zero = jnp.array(0, BF16)
    for (column_ref, gradient_ref, _), masked_ref in zip(sides, masked):
        for i, one in enumerate(turns):
            masked_ref[:, i * LANES : (i + 1) * LANES] = jnp.where(
                column_ref[...] == jnp.array(one, BF16), gradient_ref[...], zero
            )
    total = before[0][:, at * LANES : (at + len(turns)) * LANES] if before else None
    for (_, _, counts_ref), masked_ref in zip(sides, masked):
        part = jnp.dot(counts_ref[...], masked_ref[...], preferred_element_type=F32)
        total = part if total is None else total + part
    rows_ref[...] = total


def spread(turns, sides, before=None, at=0):
    bags, width = sides[0][1].shape
    rows = sides[0][2].shape[0]
    wide = len(turns) * width
    operands = [one for side in sides for one in side] + ([] if before is None else [before])
    return pl.pallas_call(
        functools.partial(spread_kernel, turns, len(sides), at),
        out_shape=jax.ShapeDtypeStruct((rows, wide), F32),
        in_specs=[VMEM] * len(operands),
        out_specs=VMEM,
        scratch_shapes=[pltpu.VMEM((bags, wide), BF16)] * len(sides),
        compiler_params=params(),
        cost_estimate=cost(0, 0),
        name="spread",
    )(*operands)


def place_kernel(at_ref, part_ref, *refs):
    rows_ref, sem = refs[-2], refs[-1]
    rows = part_ref.shape[0]
    start = pl.multiple_of(at_ref[0] * rows, rows)
    copy = pltpu.make_async_copy(part_ref, rows_ref.at[pl.ds(start, rows), :], sem)
    copy.start()
    copy.wait()


def place_half(at, part, before=None):
    rows, width = part.shape
    either = pl.BlockSpec(memory_space=pl.ANY)
    return pl.pallas_call(
        place_kernel,
        out_shape=jax.ShapeDtypeStruct((2 * rows, width), F32),
        in_specs=[pl.BlockSpec(memory_space=pltpu.SMEM), VMEM] + [either] * (before is not None),
        out_specs=either,
        scratch_shapes=[pltpu.SemaphoreType.DMA],
        input_output_aliases={} if before is None else {2: 0},
        compiler_params=params(),
        cost_estimate=cost(0, 0),
        name="place_half",
    )(at, part, *([] if before is None else [before]))


def swap(value, axis, stride):
    size = lax.axis_size(axis)
    return lax.ppermute(value, axis, [(i, i ^ stride) for i in range(size)])


def sum_pairs(value, axis, stride, wire):
    while stride < lax.axis_size(axis):
        value = value.astype(wire)
        value = value.astype(F32) + swap(value, axis, stride).astype(F32)
        stride *= 2
    return value


def ring_order(size):
    inner = 1 << ((size.bit_length() - 1) // 2)
    outer = size // inner
    cycle = []
    for far in range(outer):
        columns = range(1, inner) if far % 2 == 0 else range(inner - 1, 0, -1)
        cycle += [far * inner + column for column in columns]
    return cycle + [far * inner for far in range(outer - 1, -1, -1)]


def ring_turns(owners):
    order = ring_order(owners)
    right = []
    for group in range(lax.axis_size("grp")):
        for i in range(owners):
            here, there = order[i], order[(i + 1) % owners]
            if group % 2 == 1:
                here, there = there, here
            right.append((group * owners + here, group * owners + there))
    return right, [(there, here) for here, there in right]


def count_and_pool(where, place, shard, local_rows, ahead):
    owners = lax.axis_size("emb")
    count = lambda own: bag_counts(where, own, owners, local_rows)
    places = [place, swap(place, "grp", 1)]
    sums = [None, None]

    def add(side, turns, shards, ahead=()):
        sums[side] = pool(turns, sides[side][1], sides[side][0], shards, sums[side], ahead)

    if owners != 8:
        sides = [count(one) for one in places]
        table = lax.all_gather(shard, "emb", axis=0, tiled=False)
        for start in range(0, owners, 8):
            here = tuple(range(start, start + 8))
            for side in (1, 0):
                add(side, here, [[table[one]] for one in here])
        sums[1] = [swap(one, "grp", 1) for one in jnp.split(sums[1], 2, axis=1)]
        return sides, sums
    right, left = ring_turns(owners)
    lefts, rights = [shard], [shard]

    def step(beside):
        before = lefts[-1], rights[-1], beside
        a, b, beside = before if beside is None else lax.optimization_barrier(before)
        lefts.append(lax.ppermute(a, RING, right))
        rights.append(lax.ppermute(b, RING, left))
        return beside

    step(None)
    own, places[1] = step((count(places[0]), places[1]))
    near = (0, 1, 7), [[shard], [rights[1]], [lefts[1]]]
    *lent, sums[0] = bag_counts(
        where, places[1], owners, local_rows, near[0], (own[1], own[0]), [one for one, in near[1]]
    )
    *sides, sums[0] = step([own, lent, sums[0]])
    add(1, *near)
    add(1, (2, 6), [[rights[2]], [lefts[2]]], ahead)
    add(0, (2, 6), [[rights[2]], [lefts[2]]])
    middle = shard.shape[0] // 2
    a, b, sums[0], sums[1] = lax.optimization_barrier(
        (lefts[3][:middle], rights[3][middle:], sums[0], sums[1])
    )
    far = [lax.ppermute(a, RING, right), lax.ppermute(b, RING, left)]
    for side in (1, 0):
        add(side, (3, 5), [[rights[3]], [lefts[3]]])
    sums[0], sums[1] = lax.optimization_barrier((sums[0], sums[1]))
    turn, lent, tables = sides[1][1], sums[1], places[0].shape[0]
    sums[1] = [
        swap(pool((4,), turn, sides[1][0], [far], lent, span=span), "grp", 1)
        for span in ((0, tables // 2), (tables // 2, tables))
    ]
    add(0, (4,), [far])
    return sides, sums


def spread_and_sum(sides, grads):
    owners = lax.axis_size("emb")
    width = sides[0][1].shape[1]
    exchanges = [
        (axis, 1 << bit)
        for axis in ("grp", "emb")
        for bit in range(lax.axis_size(axis).bit_length() - 1)
    ][1:]
    if owners != 8 or len(exchanges) != 4:
        parts = [
            spread(tuple(range(start, start + 4)), sides).astype(BF16)
            for start in range(0, owners, 4)
        ]
        for axis, stride in exchanges:
            grads = grads + swap(grads, axis, stride)
        part = lax.psum_scatter(
            jnp.concatenate(parts, axis=1), "emb", scatter_dimension=1, tiled=True
        )
        return sum_pairs(part, "grp", 2, BF16), grads
    right, left = ring_turns(owners)

    def exchange(grads):
        return grads + swap(grads, *exchanges.pop(0))

    def send(to_right, to_left):
        return lax.ppermute(to_right, RING, right), lax.ppermute(to_left, RING, left)

    def messages(part, went_right, went_left):
        to_right, to_left = part[:, :width], part[:, width:]
        return (to_right + went_right).astype(BF16), (to_left + went_left).astype(BF16)

    own = spread((4, 0), sides[:1])
    part = spread((4, 0), sides[1:], own)
    far, mine = part[:, :width].astype(BF16), part[:, width:]
    middle = far.shape[0] // 2
    far, sides, grads = lax.optimization_barrier((far, sides, grads))
    went_right, went_left = send(far[:middle], far[middle:])
    went_right = jnp.pad(went_right.astype(F32), ((0, middle), (0, 0)))
    went_left = jnp.pad(went_left.astype(F32), ((middle, 0), (0, 0)))
    for step in (3, 2, 1):
        part = spread((step, owners - step), sides)
        to_right, to_left = messages(part, went_right, went_left)
        to_right, to_left, sides, grads = lax.optimization_barrier((to_right, to_left, sides, grads))
        went_right, went_left = send(to_right, to_left)
        grads = exchange(grads)
        went_right, went_left = went_right.astype(F32), went_left.astype(F32)
    total = (mine + went_right + went_left).astype(BF16)
    total, grads = lax.optimization_barrier((total, grads))
    other, grads = lax.optimization_barrier((swap(total, "grp", 2), exchange(grads)))
    return total.astype(F32) + other.astype(F32), grads


def body(
    table_window,
    dense_part,
    bag_rows,
    bag_lengths,
    bag_owner,
    labels,
    sample_weight,
    down_w,
    up_w,
    cross_bias,
    head_w,
):
    samples, tables, hot = bag_rows.shape
    local_rows, width = table_window.shape
    rows = local_rows // 2
    half = (lax.axis_index("grp") % 2).astype(jnp.int32)
    where = jnp.stack([half, lax.axis_index("emb").astype(jnp.int32)])
    shard = lax.dynamic_slice_in_dim(table_window, half * rows, rows, 0)
    shard = shard.reshape(-1, LANES, width).transpose(0, 2, 1).reshape(rows, LANES)
    live = jnp.arange(hot, dtype=jnp.int32)[None, :, None] < bag_lengths.T[:, None, :]
    place = bag_owner.transpose(1, 2, 0) * local_rows + bag_rows.transpose(1, 2, 0)
    place = jnp.where(live, place, -1)
    sides, (own, other) = count_and_pool(where, place, shard, local_rows, (down_w, up_w))
    d_pooled, dense_grad, grads = cross_layer(
        dense_part,
        own,
        *other,
        labels.astype(F32).reshape(1, samples),
        sample_weight.reshape(1, samples),
        down_w,
        up_w,
        cross_bias.reshape(-1, LANES),
        head_w.reshape(-1, LANES),
    )
    grads = grads + swap(grads, "grp", 1)
    sides = [
        (sides[0][2], d_pooled, sides[0][0]),
        (sides[1][2], swap(d_pooled, "grp", 1), sides[1][0]),
    ]
    row_half, grads = spread_and_sum(sides, grads)
    at = half.reshape(1)
    row_grad = place_half(1 - at, swap(row_half, "grp", 1), place_half(at, row_half))
    return (row_grad, grads[0].reshape(-1), grads[1].reshape(-1), dense_grad)


def solution(mesh):
    in_specs = (
        P("emb", None),
        P(("grp", "emb"), None),
        P(("grp", "emb"), None, None),
        P(("grp", "emb"), None),
        P(("grp", "emb"), None, None),
        P(("grp", "emb")),
        P(("grp", "emb")),
        P(),
        P(),
        P(),
        P(),
    )
    out_specs = (P("emb", None), P(), P(), P(("grp", "emb"), None))
    return jax.shard_map(body, mesh=mesh, in_specs=in_specs, out_specs=out_specs, check_vma=False)
```

```python
import functools

import jax
import jax.numpy as jnp
from jax import lax
from jax.experimental import pallas as pl
from jax.experimental.pallas import tpu as pltpu
from jax.sharding import PartitionSpec as P

BF16 = jnp.bfloat16
F32 = jnp.float32
LANES = 128
RING = ("grp", "emb")
CHUNK = 32
VMEM_BYTES = 16 * 1024 * 1024


def params():
    return pltpu.CompilerParams(vmem_limit_bytes=VMEM_BYTES)


VMEM = pl.BlockSpec(memory_space=pltpu.VMEM)


def cost(flops, moved):
    return pl.CostEstimate(flops=flops, bytes_accessed=moved, transcendentals=0)


def ring_place(owner):
    return jnp.where(owner % 2 == 1, owner // 2, 7 - owner // 2)


def diagonal():
    return lax.broadcasted_iota(jnp.int32, (LANES, LANES), 0) == lax.broadcasted_iota(
        jnp.int32, (LANES, LANES), 1
    )


def side_by_side(blocks):
    tiles = [ref[row : row + LANES, :] for ref in blocks for row in range(0, ref.shape[0], LANES)]
    return jnp.concatenate(tiles, axis=1)


def count_kernel(owners, local_rows, turns, where_ref, place_ref, *refs):
    if turns:
        counts_ref, turn_ref, column_ref, sum_ref = refs[-4:]
        own_turn_ref, own_counts_ref, blocks = refs[0], refs[1], refs[2:-4]
    else:
        counts_ref, turn_ref, column_ref = refs
    tables, hot, _ = place_ref.shape
    rows = counts_ref.shape[0]
    high = rows // LANES
    half, index = where_ref[0], where_ref[1]
    shift = local_rows.bit_length() - 1
    eye = diagonal()
    ones = jnp.ones((LANES, LANES), BF16)
    ids = lax.broadcasted_iota(jnp.int32, (LANES, LANES), 0)

    def table(at, carry):
        place = place_ref[at]
        owner = place[0:1, :] >> shift
        if owners == 8:
            turn = ring_place(owner) - ring_place(index)
            turn_ref[pl.ds(at, 1), :] = (jnp.where(half == 0, turn, -turn) & 7).astype(F32)
            turn = (turn & 7).astype(F32)
        else:
            turn = owner.astype(F32)
            turn_ref[pl.ds(at, 1), :] = turn
        lanes = pl.ds(pl.multiple_of(at * LANES, LANES), LANES)
        column_ref[lanes, :] = jnp.dot(
            jnp.where(eye, turn, 0.0).astype(BF16), ones, preferred_element_type=F32
        ).astype(BF16)
        here = (place & (local_rows - 1)) - half * rows
        inside = (place >= 0) & (here >= 0) & (here < rows)
        low = jnp.where(inside, here & (LANES - 1), -1)
        code = jnp.where(inside, jnp.left_shift(1, 4 * (here >> (LANES.bit_length() - 1))), 0)
        for first in range(0, LANES, CHUNK):
            total = 0
            for h in range(hot):
                total = total + jnp.where(
                    ids[first : first + CHUNK] == low[h : h + 1, :], code[h : h + 1, :], 0
                )
            for part in range(high):
                count = lax.shift_right_logical(total, 4 * part) & 15
                start = part * LANES + first
                counts_ref[start : start + CHUNK, lanes] = count.astype(F32).astype(BF16)
        return carry

    def pair(at, carry):
        lanes = pl.ds(pl.multiple_of(at * 2 * LANES, 2 * LANES), 2 * LANES)
        left = jnp.concatenate([side_by_side([block]) for block in blocks], axis=0)
        product = jnp.dot(left, own_counts_ref[:, lanes], preferred_element_type=F32)
        for one in range(2):
            table(2 * at + one, 0)
        total = []
        for one in range(2):
            turn = own_turn_ref[pl.ds(2 * at + one, 1), :]
            part = 0.0
            for i, each in enumerate(turns):
                mine = product[i * LANES : (i + 1) * LANES, one * LANES : (one + 1) * LANES]
                part = jnp.where(turn == each, mine, part)
            total.append(part)
        sum_ref[:, lanes] = jnp.concatenate(total, axis=1)
        return carry

    if turns:
        lax.fori_loop(0, tables // 2, pair, 0)
    else:
        lax.fori_loop(0, tables, table, 0, unroll=2)


def bag_counts(where, place, owners, local_rows, turns=(), own=(), shards=()):
    tables, hot, samples = place.shape
    bags = tables * samples
    rows = local_rows // 2
    operands = [*own, *shards] if turns else []
    out_shape = (
        jax.ShapeDtypeStruct((rows, bags), BF16),
        jax.ShapeDtypeStruct((tables, samples), F32),
        jax.ShapeDtypeStruct((bags, LANES), BF16),
    ) + ((jax.ShapeDtypeStruct((LANES, bags), F32),) if turns else ())
    return pl.pallas_call(
        functools.partial(count_kernel, owners, local_rows, turns),
        out_shape=out_shape,
        in_specs=[pl.BlockSpec(memory_space=pltpu.SMEM)] + [VMEM] * (1 + len(operands)),
        out_specs=(VMEM,) * len(out_shape),
        compiler_params=params(),
        cost_estimate=cost(5 * 10**9, 0),
        name="bag_counts",
    )(where, place, *operands)


def pool_kernel(shards, turns, tables, added, span, turn_ref, counts_ref, *refs):
    sum_ref = refs[-1]
    blocks = refs[: sum(shards)]
    before = refs[sum(shards) : sum(shards) + added]
    left, at = [], 0
    for parts in shards:
        left.append(side_by_side(blocks[at : at + parts]))
        at += parts
    left = jnp.concatenate(left, axis=0)
    for start in range(*span, tables):
        bags = slice(start * LANES, (start + tables) * LANES)
        product = jnp.dot(left, counts_ref[:, bags], preferred_element_type=F32)
        for table in range(tables):
            turn = turn_ref[start + table : start + table + 1, :]
            here = slice((start + table) * LANES, (start + table + 1) * LANES)
            total = before[0][:, here] if before else 0.0
            for i, one in enumerate(turns):
                mine = product[i * LANES : (i + 1) * LANES, table * LANES : (table + 1) * LANES]
                total = jnp.where(turn == one, mine, total)
            place = start + table - span[0]
            sum_ref[:, place * LANES : (place + 1) * LANES] = total


def pool(turns, turn, counts, shards, before, ahead=(), span=None):
    rows, bags = counts.shape
    blocks = [block for shard in shards for block in shard]
    width = blocks[0].shape[1]
    first, last = span or (0, turn.shape[0])
    extra = ([] if before is None else [before]) + list(ahead)
    return pl.pallas_call(
        functools.partial(
            pool_kernel,
            [len(shard) for shard in shards],
            turns,
            (last - first) if len(turns) <= 4 else (last - first) // 2,
            0 if before is None else 1,
            (first, last),
        ),
        out_shape=jax.ShapeDtypeStruct((width, (last - first) * LANES), F32),
        in_specs=[VMEM] * (2 + len(blocks) + len(extra)),
        out_specs=VMEM,
        compiler_params=params(),
        cost_estimate=cost(0, 0),
        name="pool",
    )(turn, counts, *blocks, *extra)


def cross_kernel(
    tables,
    dense_ref,
    own_ref,
    first_ref,
    second_ref,
    label_ref,
    weight_ref,
    down_ref,
    up_ref,
    bias_ref,
    head_ref,
    d_pooled_ref,
    dense_grad_ref,
    grads_ref,
    x0_ref,
    cross_ref,
    d_cross_ref,
):
    samples = dense_ref.shape[0]
    blocks = tables + 1
    eye = diagonal()
    column = lambda ref: jnp.sum(jnp.where(eye, ref[...], 0.0), axis=1, keepdims=True)
    x0_ref[:, :LANES] = dense_ref[...]
    for table in range(tables):
        here = slice(table * LANES, (table + 1) * LANES)
        part, start = (first_ref, 0) if table < tables // 2 else (second_ref, tables // 2)
        other = part[:, (table - start) * LANES : (table - start + 1) * LANES]
        x0_ref[:, (table + 1) * LANES : (table + 2) * LANES] = (
            (own_ref[:, here] + other).T.astype(BF16)
        )
    low = jnp.dot(x0_ref[...], down_ref[...], preferred_element_type=F32).astype(BF16)
    logit = jnp.zeros((samples, LANES), F32)
    for block in range(blocks):
        here = slice(block * LANES, (block + 1) * LANES)
        cross = jnp.dot(low, up_ref[:, here], preferred_element_type=F32) + bias_ref[block : block + 1, :]
        cross_ref[:, here] = cross
        x0f = x0_ref[:, here].astype(F32)
        logit = logit + (x0f * cross + x0f) * head_ref[block : block + 1, :]
    logit = jnp.sum(logit, axis=1, keepdims=True)
    d_logit = column(weight_ref) * (jax.nn.sigmoid(logit) - column(label_ref))
    for block in range(blocks):
        here = slice(block * LANES, (block + 1) * LANES)
        x0f = x0_ref[:, here].astype(F32)
        x1 = x0f * cross_ref[:, here] + x0f
        grads_ref[0, block : block + 1, :] = jnp.sum(d_logit * x1, axis=0, keepdims=True)
        d_cross = d_logit * head_ref[block : block + 1, :] * x0f
        grads_ref[1, block : block + 1, :] = jnp.sum(d_cross, axis=0, keepdims=True)
        d_cross_ref[:, here] = d_cross.astype(BF16)
    d_low = lax.dot_general(
        d_cross_ref[...], up_ref[...], (((1,), (1,)), ((), ())), preferred_element_type=F32
    ).astype(BF16)
    for block in range(blocks):
        here = slice(block * LANES, (block + 1) * LANES)
        d_x1 = d_logit * head_ref[block : block + 1, :]
        d_x0 = d_x1 * (cross_ref[:, here] + 1.0) + lax.dot_general(
            d_low, down_ref[here, :], (((1,), (1,)), ((), ())), preferred_element_type=F32
        )
        if block == 0:
            dense_grad_ref[...] = d_x0.astype(BF16)
        else:
            place = slice((block - 1) * samples, block * samples)
            d_pooled_ref[place, :] = d_x0.astype(BF16)


def cross_layer(dense, own, first, second, labels, weights, down_w, up_w, bias, head):
    samples, width = dense.shape
    tables = own.shape[1] // samples
    cross = down_w.shape[0]
    return pl.pallas_call(
        functools.partial(cross_kernel, tables),
        out_shape=(
            jax.ShapeDtypeStruct((tables * samples, width), BF16),
            jax.ShapeDtypeStruct((samples, width), BF16),
            jax.ShapeDtypeStruct((2, cross // LANES, LANES), F32),
        ),
        scratch_shapes=[
            pltpu.VMEM((samples, cross), BF16),
            pltpu.VMEM((samples, cross), F32),
            pltpu.VMEM((samples, cross), BF16),
        ],
        compiler_params=params(),
        cost_estimate=cost(8 * 10**9, 12 * 10**6),
        name="cross_layer",
    )(dense, own, first, second, labels, weights, down_w, up_w, bias, head)


def spread_kernel(turns, count, at, *refs):
    sides = [refs[3 * i : 3 * i + 3] for i in range(count)]
    before = refs[3 * count : -1 - count]
    rows_ref, masked = refs[-1 - count], refs[-count:]
    zero = jnp.array(0, BF16)
    for (column_ref, gradient_ref, _), masked_ref in zip(sides, masked):
        for i, one in enumerate(turns):
            masked_ref[:, i * LANES : (i + 1) * LANES] = jnp.where(
                column_ref[...] == jnp.array(one, BF16), gradient_ref[...], zero
            )
    total = before[0][:, at * LANES : (at + len(turns)) * LANES] if before else None
    for (_, _, counts_ref), masked_ref in zip(sides, masked):
        part = jnp.dot(counts_ref[...], masked_ref[...], preferred_element_type=F32)
        total = part if total is None else total + part
    rows_ref[...] = total


def spread(turns, sides, before=None, at=0):
    bags, width = sides[0][1].shape
    rows = sides[0][2].shape[0]
    wide = len(turns) * width
    operands = [one for side in sides for one in side] + ([] if before is None else [before])
    return pl.pallas_call(
        functools.partial(spread_kernel, turns, len(sides), at),
        out_shape=jax.ShapeDtypeStruct((rows, wide), F32),
        in_specs=[VMEM] * len(operands),
        out_specs=VMEM,
        scratch_shapes=[pltpu.VMEM((bags, wide), BF16)] * len(sides),
        compiler_params=params(),
        cost_estimate=cost(0, 0),
        name="spread",
    )(*operands)


def place_kernel(at_ref, part_ref, *refs):
    rows_ref, sem = refs[-2], refs[-1]
    rows = part_ref.shape[0]
    start = pl.multiple_of(at_ref[0] * rows, rows)
    copy = pltpu.make_async_copy(part_ref, rows_ref.at[pl.ds(start, rows), :], sem)
    copy.start()
    copy.wait()


def place_half(at, part, before=None):
    rows, width = part.shape
    either = pl.BlockSpec(memory_space=pl.ANY)
    return pl.pallas_call(
        place_kernel,
        out_shape=jax.ShapeDtypeStruct((2 * rows, width), F32),
        in_specs=[pl.BlockSpec(memory_space=pltpu.SMEM), VMEM] + [either] * (before is not None),
        out_specs=either,
        scratch_shapes=[pltpu.SemaphoreType.DMA],
        input_output_aliases={} if before is None else {2: 0},
        compiler_params=params(),
        cost_estimate=cost(0, 0),
        name="place_half",
    )(at, part, *([] if before is None else [before]))


def swap(value, axis, stride):
    size = lax.axis_size(axis)
    return lax.ppermute(value, axis, [(i, i ^ stride) for i in range(size)])


def sum_pairs(value, axis, stride, wire):
    while stride < lax.axis_size(axis):
        value = value.astype(wire)
        value = value.astype(F32) + swap(value, axis, stride).astype(F32)
        stride *= 2
    return value


def ring_order(size):
    inner = 1 << ((size.bit_length() - 1) // 2)
    outer = size // inner
    cycle = []
    for far in range(outer):
        columns = range(1, inner) if far % 2 == 0 else range(inner - 1, 0, -1)
        cycle += [far * inner + column for column in columns]
    return cycle + [far * inner for far in range(outer - 1, -1, -1)]


def ring_turns(owners, opposite):
    order = ring_order(owners)
    right = []
    for group in range(lax.axis_size("grp")):
        for i in range(owners):
            here, there = order[i], order[(i + 1) % owners]
            if opposite and group % 2 == 1:
                here, there = there, here
            right.append((group * owners + here, group * owners + there))
    return right, [(there, here) for here, there in right]


def count_and_pool(where, place, shard, local_rows, ahead):
    owners = lax.axis_size("emb")
    count = lambda own: bag_counts(where, own, owners, local_rows)
    places = [place, swap(place, "grp", 1)]
    sums = [None, None]

    def add(side, turns, shards, ahead=()):
        sums[side] = pool(turns, sides[side][1], sides[side][0], shards, sums[side], ahead)

    if owners != 8:
        sides = [count(one) for one in places]
        table = lax.all_gather(shard, "emb", axis=0, tiled=False)
        for start in range(0, owners, 8):
            here = tuple(range(start, start + 8))
            for side in (1, 0):
                add(side, here, [[table[one]] for one in here])
        sums[1] = [swap(one, "grp", 1) for one in jnp.split(sums[1], 2, axis=1)]
        return sides, sums
    right, left = ring_turns(owners, True)
    lefts, rights = [shard], [shard]

    def step(beside):
        before = lefts[-1], rights[-1], beside
        a, b, beside = before if beside is None else lax.optimization_barrier(before)
        lefts.append(lax.ppermute(a, RING, right))
        rights.append(lax.ppermute(b, RING, left))
        return beside

    step(None)
    own, places[1] = step((count(places[0]), places[1]))
    near = (0, 1, 7), [[shard], [rights[1]], [lefts[1]]]
    *lent, sums[0] = bag_counts(
        where, places[1], owners, local_rows, near[0], (own[1], own[0]), [one for one, in near[1]]
    )
    *sides, sums[0] = step([own, lent, sums[0]])
    add(1, *near)
    add(1, (2, 6), [[rights[2]], [lefts[2]]], ahead)
    add(0, (2, 6), [[rights[2]], [lefts[2]]])
    middle = shard.shape[0] // 2
    a, b, sums[0], sums[1] = lax.optimization_barrier(
        (lefts[3][:middle], rights[3][middle:], sums[0], sums[1])
    )
    far = [lax.ppermute(a, RING, right), lax.ppermute(b, RING, left)]
    for side in (1, 0):
        add(side, (3, 5), [[rights[3]], [lefts[3]]])
    sums[0], sums[1] = lax.optimization_barrier((sums[0], sums[1]))
    turn, lent, tables = sides[1][1], sums[1], places[0].shape[0]
    sums[1] = [
        swap(pool((4,), turn, sides[1][0], [far], lent, span=span), "grp", 1)
        for span in ((0, tables // 2), (tables // 2, tables))
    ]
    add(0, (4,), [far])
    return sides, sums


def spread_and_sum(sides, grads):
    owners = lax.axis_size("emb")
    width = sides[0][1].shape[1]
    exchanges = [
        (axis, 1 << bit)
        for axis in ("grp", "emb")
        for bit in range(lax.axis_size(axis).bit_length() - 1)
    ][1:]
    if owners != 8 or len(exchanges) != 4:
        parts = [
            spread(tuple(range(start, start + 4)), sides).astype(BF16)
            for start in range(0, owners, 4)
        ]
        for axis, stride in exchanges:
            grads = grads + swap(grads, axis, stride)
        part = lax.psum_scatter(
            jnp.concatenate(parts, axis=1), "emb", scatter_dimension=1, tiled=True
        )
        return sum_pairs(part, "grp", 2, BF16), grads
    right, left = ring_turns(owners, False)

    def exchange(grads):
        return grads + swap(grads, *exchanges.pop(0))

    def send(to_right, to_left):
        return lax.ppermute(to_right, RING, right), lax.ppermute(to_left, RING, left)

    def messages(part, went_right, went_left):
        to_right, to_left = part[:, :width], part[:, width:]
        return (to_right + went_right).astype(BF16), (to_left + went_left).astype(BF16)

    own = spread((4, 0), sides[:1])
    part = spread((4, 0), sides[1:], own)
    far, mine = part[:, :width].astype(BF16), part[:, width:]
    middle = far.shape[0] // 2
    far, sides, grads = lax.optimization_barrier((far, sides, grads))
    went_right, went_left = send(far[:middle], far[middle:])
    went_right = jnp.pad(went_right.astype(F32), ((0, middle), (0, 0)))
    went_left = jnp.pad(went_left.astype(F32), ((middle, 0), (0, 0)))
    for step in (3, 2, 1):
        part = spread((step, owners - step), sides)
        to_right, to_left = messages(part, went_right, went_left)
        to_right, to_left, sides, grads = lax.optimization_barrier((to_right, to_left, sides, grads))
        went_right, went_left = send(to_right, to_left)
        grads = exchange(grads)
        went_right, went_left = went_right.astype(F32), went_left.astype(F32)
    total = (mine + went_right + went_left).astype(BF16)
    total, grads = lax.optimization_barrier((total, grads))
    other, grads = lax.optimization_barrier((swap(total, "grp", 2), exchange(grads)))
    return total.astype(F32) + other.astype(F32), grads


def body(
    table_window,
    dense_part,
    bag_rows,
    bag_lengths,
    bag_owner,
    labels,
    sample_weight,
    down_w,
    up_w,
    cross_bias,
    head_w,
):
    samples, tables, hot = bag_rows.shape
    local_rows, width = table_window.shape
    rows = local_rows // 2
    half = (lax.axis_index("grp") % 2).astype(jnp.int32)
    where = jnp.stack([half, lax.axis_index("emb").astype(jnp.int32)])
    shard = lax.dynamic_slice_in_dim(table_window, half * rows, rows, 0)
    shard = shard.reshape(-1, LANES, width).transpose(0, 2, 1).reshape(rows, LANES)
    live = jnp.arange(hot, dtype=jnp.int32)[None, :, None] < bag_lengths.T[:, None, :]
    place = bag_owner.transpose(1, 2, 0) * local_rows + bag_rows.transpose(1, 2, 0)
    place = jnp.where(live, place, -1)
    sides, (own, other) = count_and_pool(where, place, shard, local_rows, (down_w, up_w))
    d_pooled, dense_grad, grads = cross_layer(
        dense_part,
        own,
        *other,
        labels.astype(F32).reshape(1, samples),
        sample_weight.reshape(1, samples),
        down_w,
        up_w,
        cross_bias.reshape(-1, LANES),
        head_w.reshape(-1, LANES),
    )
    grads = grads + swap(grads, "grp", 1)
    sides = [
        (sides[0][2], d_pooled, sides[0][0]),
        (sides[1][2], swap(d_pooled, "grp", 1), sides[1][0]),
    ]
    row_half, grads = spread_and_sum(sides, grads)
    at = half.reshape(1)
    row_grad = place_half(1 - at, swap(row_half, "grp", 1), place_half(at, row_half))
    return (row_grad, grads[0].reshape(-1), grads[1].reshape(-1), dense_grad)


def solution(mesh):
    in_specs = (
        P("emb", None),
        P(("grp", "emb"), None),
        P(("grp", "emb"), None, None),
        P(("grp", "emb"), None),
        P(("grp", "emb"), None, None),
        P(("grp", "emb")),
        P(("grp", "emb")),
        P(),
        P(),
        P(),
        P(),
    )
    out_specs = (P("emb", None), P(), P(), P(("grp", "emb"), None))
    return jax.shard_map(body, mesh=mesh, in_specs=in_specs, out_specs=out_specs, check_vma=False)
```
